128 devices in a mesh: dp: 32 (over z, x, core), grp: 4 (over y).
Axes of the slice: x: 4, y: 4, z: 4, core: 2. Of those that a mesh axis runs over, the one named last changes fastest.
Arguments:
- queries: bfloat16 [256, 4, 128, 576], P(('dp', 'grp')), may hold values from -64 to 64
- new_latent: bfloat16 [256, 4, 576], P(('dp', 'grp')), may hold values from -8 to 8
- latent_cache: bfloat16 [8192, 64, 576], P(('dp', 'grp')), may hold values from -6 to 6
- block_table: int32 [256, 32], P(('dp', 'grp')), may hold values from 0 to 63, as said below
- lengths: int32 [256], replicated, may hold values from 1 to 2048, as said below
- migration: int32 [128], replicated, may hold values from 0 to 1
- residual: bfloat16 [256, 4, 7168], P('dp', None, 'grp'), may hold values from -10 to 10
- value_projection_weight: bfloat16 [128, 512, 128], P('dp'), may hold values from -2 to 2
- output_proj: bfloat16 [16384, 7168], P('dp', 'grp'), may hold values from -0.046875 to 0.046875
- norm_gain: bfloat16 [7168], P('grp'), may hold values from 0.25 to 1.75
- gate_proj: bfloat16 [7168, 18432], P('grp', 'dp'), may hold values from -0.0625 to 0.0625
- up_proj: bfloat16 [7168, 18432], P('grp', 'dp'), may hold values from -0.0625 to 0.0625
- down_projection_matrix: bfloat16 [18432, 7168], P('dp', 'grp'), may hold values from -0.046875 to 0.046875
Outputs:
- layer_out: bfloat16 [256, 4, 7168], P('dp', None, 'grp')
The draws below stay inside these ranges and needn't reach their ends.
Inputs may be any that keep to these rules, and one draw needn't show every extreme that they name: `lengths`: some row has exactly 2048 cached tokens. `block_table`: the rows of one device together name each of its 64 pages exactly once.
All inputs are finite; a program needn't handle non-finite values.
Results may differ from the reference program's by a relative error of at most 0.007.
Values may be sent and summed in bfloat16 or wider, within the bound.
No kernel may reach another device: no remote copies, remote signals or barrier semaphores. Data moves between devices by JAX's collectives and lax.ppermute only.
A program may use at most 128 MiB of HBM per device.

```python
import jax
import jax.numpy as jnp
from jax import lax

D = 7168
H = 128
KV = 512
ROPE = 64
VH = 128
FF = 18432
PAGE = 64
STEPS = 4
MAXP = 32
ROWS_DEV = 2
ROWS = 256
PAGES_DEV = 64
PAGES = 8192
N_DP = 32
N_GRP = 4
DEVICES = 128


def row_loads(key):
    half_count = N_DP // 2
    heavy_half = jax.random.randint(jax.random.fold_in(key, 101), (half_count, N_GRP), 0, 2)
    heavy_side = jnp.concatenate([heavy_half, 1 - heavy_half], axis=0).reshape(-1)
    heavy_rows = jnp.repeat(heavy_side, ROWS_DEV)
    most_tokens = MAXP * PAGE
    long_len = jax.random.randint(jax.random.fold_in(key, 102), (ROWS,), most_tokens // 2, most_tokens + 1)
    short_len = jax.random.randint(jax.random.fold_in(key, 103), (ROWS,), 1, max(most_tokens // 4, 1) + 1)
    longest_row = jax.random.randint(jax.random.fold_in(key, 104), (), 0, ROWS)
    lengths = jnp.where(heavy_rows == 1, long_len, short_len)
    lengths = jnp.where(jnp.arange(ROWS) == longest_row, most_tokens, lengths).astype(jnp.int32)
    per_device = lengths.reshape(-1, ROWS_DEV)
    migration = jnp.where(heavy_side == 1, jnp.argmax(per_device, axis=1), jnp.argmin(per_device, axis=1))
    return (lengths, migration.astype(jnp.int32))


def draw_lengths(key, part):
    lengths, migration = row_loads(key)
    return lengths


def draw_migration(key, part):
    lengths, migration = row_loads(key)
    return migration


def draw_block_table(key, part):
    key = jax.random.fold_in(key, 7)
    device_keys = jax.random.split(key, N_DP * N_GRP)
    orders = jax.vmap(lambda one_key: jax.random.permutation(one_key, PAGES_DEV))(device_keys)
    return orders.reshape(ROWS, MAXP).astype(jnp.int32)


def latent_pair(key, tie):
    width = KV + ROPE
    fresh = jax.random.truncated_normal(jax.random.fold_in(key, 201), -6.0, 6.0, (ROWS, STEPS, width), jnp.float32)
    fresh = fresh.at[:, 1].set(fresh[:, 1])
    queries = jax.random.truncated_normal(jax.random.fold_in(key, 203), -6.0, 6.0, (ROWS, STEPS, H, width), jnp.float32)
    chosen = (jax.random.randint(jax.random.fold_in(key, 204), (ROWS, 1, H, 1), 0, 16) == 0).astype(jnp.float32) * tie
    queries = queries * (1.0 - chosen)
    return (queries, fresh)


def draw_queries(key, part):
    tie = 0.0
    queries, fresh = latent_pair(key, tie)
    return queries.astype(jnp.bfloat16)


def draw_new_latent(key, part):
    tie = 0.0
    queries, fresh = latent_pair(key, tie)
    return fresh.astype(jnp.bfloat16)


def draw_residual(key, part):
    key = jax.random.fold_in(key, 9)
    base = jax.random.truncated_normal(jax.random.fold_in(key, 1), -6.0, 6.0, (ROWS, STEPS, D), jnp.float32)
    row_scale = jnp.exp(jax.random.uniform(jax.random.fold_in(key, 2), (ROWS, STEPS, 1), jnp.float32, -1.15, 1.15))
    column_scale = 3.0 ** (jnp.arange(D, dtype=jnp.float32) / D) / 6.8
    return (base * row_scale * column_scale).astype(jnp.bfloat16)


def level_of(stream_key, extent, pieces, low, largest):
    gain = 1.0
    for dim, blocks in pieces:
        draws = jax.random.uniform(jax.random.fold_in(jax.random.fold_in(stream_key, 6), dim), (blocks,), jnp.float32, low / len(pieces), largest / len(pieces))
        gain = gain * jnp.repeat(jnp.exp(draws), extent[dim] // blocks).reshape((-1,) + (1,) * (len(extent) - 1 - dim))
    return gain


def noise(rng, shape, scale, most, cuts=(), kind=jnp.bfloat16):
    entries = jax.random.normal(rng, shape, jnp.float32) * scale
    if len(cuts) > 0:
        entries = level_of(rng, shape, cuts, -0.22, 0.18) * entries
    return jnp.clip(entries, min=-most, max=most).astype(kind)


def setup_inputs(seed: int = 0) -> dict:
    key_list = jax.random.split(jax.random.key(seed), 14)
    return {
        "queries": draw_queries(jax.random.fold_in(key_list[13], 71), 0),
        "new_latent": draw_new_latent(jax.random.fold_in(key_list[13], 71), 0),
        "latent_cache": noise(key_list[2], (PAGES, PAGE, KV + ROPE), 1.0, 6.0, ((0, 128),)),
        "block_table": draw_block_table(jax.random.fold_in(key_list[13], 71), 0),
        "lengths": draw_lengths(jax.random.fold_in(key_list[13], 71), 0),
        "migration": draw_migration(jax.random.fold_in(key_list[13], 71), 0),
        "residual": draw_residual(jax.random.fold_in(key_list[13], 71), 0),
        "value_projection_weight": noise(key_list[7], (H, KV, VH), (KV // 64) ** -0.5, 2.0, ((0, 32),)),
        "output_proj": noise(key_list[8], (H * VH, D), (H * VH) ** -0.5, 0.046875, ((0, 32), (1, 4))),
        "norm_gain": jnp.clip(1.0 + 0.15 * jax.random.normal(key_list[9], (D,), jnp.float32), 0.25, 1.75).astype(jnp.bfloat16),
        "gate_proj": noise(key_list[10], (D, FF), D ** -0.5, 0.0625, ((0, 4), (1, 32))),
        "up_proj": noise(key_list[11], (D, FF), D ** -0.5, 0.0625, ((0, 4), (1, 32))),
        "down_projection_matrix": noise(key_list[12], (FF, D), FF ** -0.5, 0.046875, ((0, 32), (1, 4))),
    }


score_scale = 0.07216878364870323
tiny_eps = 1e-06
neg_fill = -1e+30

def slot_rows(migration):
    slot_ids = jnp.arange(ROWS, dtype=jnp.int32)
    device = slot_ids // ROWS_DEV
    within = slot_ids % ROWS_DEV
    partner = (device + N_DP // 2 * N_GRP) % DEVICES
    moved_slot = within == migration[device]
    return jnp.where(moved_slot, partner * ROWS_DEV + migration[partner], slot_ids).astype(jnp.int32)

def attend(query_rows, fresh_keys, key_rows, length):
    step_count = query_rows.shape[0]
    head_count = query_rows.shape[1]
    query_flat = query_rows.reshape(step_count * head_count, query_rows.shape[2])
    past_scores = jnp.dot(query_flat, key_rows.T, preferred_element_type=jnp.float32) * score_scale
    valid_keys = jnp.arange(key_rows.shape[0], dtype=jnp.int32) < length
    past_scores = jnp.where(valid_keys[None, :], past_scores, neg_fill)
    own_scores = jnp.einsum('thc,sc->ths', query_rows.astype(jnp.float32), fresh_keys.astype(jnp.float32)) * score_scale
    causal = jnp.arange(step_count)[None, :] <= jnp.arange(step_count)[:, None]
    own_scores = jnp.where(causal[:, None, :], own_scores, neg_fill).reshape(step_count * head_count, step_count)
    row_max = jnp.maximum(lax.optimization_barrier(jnp.max(past_scores, axis=1)), lax.optimization_barrier(jnp.max(own_scores, axis=1)))
    past_weight = jnp.exp(past_scores - row_max[:, None])
    own_weight = jnp.exp(own_scores - row_max[:, None])
    row_total = lax.optimization_barrier(jnp.sum(past_weight, axis=1)) + lax.optimization_barrier(jnp.sum(own_weight, axis=1))
    past_probs = (past_weight / row_total[:, None]).astype(jnp.bfloat16)
    own_probs = (own_weight / row_total[:, None]).astype(jnp.bfloat16)
    result = jnp.dot(past_probs, key_rows[:, :KV], preferred_element_type=jnp.float32)
    result = result + jnp.dot(own_probs, fresh_keys[:, :KV], preferred_element_type=jnp.float32)
    return result.reshape(step_count, head_count, KV).astype(jnp.bfloat16)

def reference(queries, new_latent, latent_cache, block_table, lengths, migration, residual, value_projection_weight, output_proj, norm_gain, gate_proj, up_proj, down_projection_matrix):
    row_of_slot = slot_rows(migration)

    def one_slot(inputs):
        query_rows, fresh_keys, row_id = inputs
        page_ids = row_id // ROWS_DEV * PAGES_DEV + block_table[row_id]
        key_rows = latent_cache[page_ids].reshape(MAXP * PAGE, KV + ROPE)
        return attend(query_rows, fresh_keys, key_rows, lengths[row_id])
    latent_output = lax.map(one_slot, (queries, new_latent, row_of_slot))
    per_head_output = jnp.einsum('pusj,sjf->pusf', latent_output.astype(jnp.float32), value_projection_weight.astype(jnp.float32)).astype(jnp.bfloat16)
    head_flat = per_head_output.reshape(ROWS * STEPS, H * VH)
    attn_out = jnp.dot(head_flat, output_proj, preferred_element_type=jnp.float32).reshape(ROWS, STEPS, D)
    mixed_rows = residual.astype(jnp.float32) + attn_out
    square_mean = lax.optimization_barrier(jnp.mean(mixed_rows * mixed_rows, axis=2, keepdims=True))
    normalized_input = (mixed_rows * lax.rsqrt(square_mean + tiny_eps) * norm_gain.astype(jnp.float32)).astype(jnp.bfloat16)
    normed_flat = normalized_input.reshape(ROWS * STEPS, D)
    gate_sum = jnp.dot(normed_flat, gate_proj, preferred_element_type=jnp.float32)
    up_sum = jnp.dot(normed_flat, up_proj, preferred_element_type=jnp.float32)
    hidden = (jax.nn.silu(gate_sum) * up_sum).astype(jnp.bfloat16)
    down_sum = jnp.dot(hidden, down_projection_matrix, preferred_element_type=jnp.float32).reshape(ROWS, STEPS, D)
    return (mixed_rows + down_sum).astype(jnp.bfloat16)
```

```python
import functools

import jax
import jax.numpy as jnp
from jax import lax
from jax.experimental import pallas as pl
from jax.experimental.pallas import tpu as pltpu
from jax.sharding import PartitionSpec as P

D = 7168
KV = 512
KW = 576
PAGE = 64
MAXP = 32
STEPS = 4
HEADS = 128
TOKENS = PAGE * MAXP
CHUNK = 512
KEYS = TOKENS + 128
QROWS = STEPS * HEADS
CHIPS = 16
DCOL = D // 4
HALF = DCOL // 2
FFW = 1152
GW = 2 * FFW + 128

score_scale = 0.07216878364870323
exp2_scale = score_scale * 1.4426950408889634
tiny_eps = 1e-06
neg_fill = -1e30

BF = jnp.bfloat16
F32 = jnp.float32
VMEM = pl.BlockSpec(memory_space=pltpu.VMEM)
SMEM = pl.BlockSpec(memory_space=pltpu.SMEM)
ANY = pl.BlockSpec(memory_space=pl.ANY)


def params(mb=48):
    return pltpu.CompilerParams(vmem_limit_bytes=mb * 1024 * 1024)


def shape(dims, kind=BF):
    return jax.ShapeDtypeStruct(dims, kind)


def dot(a, b):
    return jnp.dot(a, b, preferred_element_type=F32)


def dot_t(a, b):
    return lax.dot_general(a, b, (((1,), (1,)), ((), ())), preferred_element_type=F32)


def pack_body(ids, mig, q_ref, f_ref, o_ref):
    o_ref[0, 0:QROWS, :] = q_ref[0]
    o_ref[0, QROWS : QROWS + 16, :] = f_ref[0]


def pack(ids, migration, queries, fresh):
    return pl.pallas_call(
        pack_body,
        out_shape=shape((1, QROWS + 16, KW)),
        grid_spec=pltpu.PrefetchScalarGridSpec(
            num_scalar_prefetch=2,
            grid=(1,),
            in_specs=[
                pl.BlockSpec((1, QROWS, KW), lambda i, ids, mig: (mig[ids[4]], 0, 0)),
                pl.BlockSpec((1, 16, KW), lambda i, ids, mig: (mig[ids[4]], 0, 0)),
            ],
            out_specs=pl.BlockSpec((1, QROWS + 16, KW), lambda i, ids, mig: (0, 0, 0)),
        ),
        compiler_params=params(),
    )(ids, migration, queries, fresh)


def attend_body(moved, ids, mig, table, lengths, q_ref, f_ref, cache, o_ref, kbuf, s_ref, m_ref, l_ref, a_ref, sems):
    own = mig[ids[4]]
    row = own if moved else 1 - own
    length = lengths[ids[4] * 2 + row]
    copies = []
    for i in range(MAXP):
        copy = pltpu.make_async_copy(
            cache.at[table[row, i]], kbuf.at[pl.ds(i * PAGE, PAGE), :], sems.at[i]
        )
        copy.start()
        copies.append(copy)
    kbuf[TOKENS : TOKENS + 16, :] = f_ref[0]
    kbuf[TOKENS + 16 :, :] = jnp.zeros((KEYS - TOKENS - 16, KW), BF)
    q = q_ref[0]
    step = lax.broadcasted_iota(jnp.int32, (QROWS, 128), 0) // HEADS
    place = lax.broadcasted_iota(jnp.int32, (QROWS, 128), 1)
    fresh = jnp.where(place <= step, dot_t(q, kbuf[TOKENS:, :]), neg_fill)
    s_ref[:, TOKENS:] = fresh
    m_ref[...] = fresh
    for c in range(TOKENS // CHUNK):
        for i in range(c * CHUNK // PAGE, (c + 1) * CHUNK // PAGE):
            copies[i].wait()

        @pl.when(c * CHUNK < length)
        def _():
            scores = dot_t(q, kbuf[c * CHUNK : (c + 1) * CHUNK, :])
            key = lax.broadcasted_iota(jnp.int32, (QROWS, CHUNK), 1) + c * CHUNK
            scores = jnp.where(key < length, scores, neg_fill)
            s_ref[:, c * CHUNK : (c + 1) * CHUNK] = scores
            best = m_ref[...]
            for k in range(CHUNK // 128):
                best = jnp.maximum(best, scores[:, k * 128 : (k + 1) * 128])
            m_ref[...] = best

    top = jnp.max(m_ref[...], axis=1, keepdims=True)
    m_ref[...] = jnp.broadcast_to(top, (QROWS, 128))
    weight = jnp.exp2((s_ref[:, TOKENS:] - top) * exp2_scale)
    l_ref[...] = weight
    a_ref[...] = dot(weight.astype(BF), kbuf[TOKENS:, :KV])
    for c in range(TOKENS // CHUNK):

        @pl.when(c * CHUNK < length)
        def _():
            top = m_ref[:, 0:1]
            weight = jnp.exp2((s_ref[:, c * CHUNK : (c + 1) * CHUNK] - top) * exp2_scale)
            total = l_ref[...]
            for k in range(CHUNK // 128):
                total = total + weight[:, k * 128 : (k + 1) * 128]
            l_ref[...] = total
            a_ref[...] += dot(weight.astype(BF), kbuf[c * CHUNK : (c + 1) * CHUNK, :KV])

    out = a_ref[...] / jnp.sum(l_ref[...], axis=1, keepdims=True)
    for k in range(CHIPS):
        parts = [out[t * HEADS + k * 8 : t * HEADS + k * 8 + 8] for t in range(STEPS)]
        o_ref[k] = jnp.concatenate(parts, axis=0).astype(BF)


def attend(moved, ids, migration, table, lengths, queries, fresh, cache):
    if moved:
        q_map = lambda i, ids, mig, tab, lens: (0, 0, 0)
        f_map = lambda i, ids, mig, tab, lens: (0, QROWS // 16, 0)
    else:
        q_map = f_map = lambda i, ids, mig, tab, lens: (1 - mig[ids[4]], 0, 0)
    return pl.pallas_call(
        functools.partial(attend_body, moved),
        out_shape=shape((CHIPS, 32, KV)),
        grid_spec=pltpu.PrefetchScalarGridSpec(
            num_scalar_prefetch=4,
            grid=(1,),
            in_specs=[
                pl.BlockSpec((1, QROWS, KW), q_map),
                pl.BlockSpec((1, 16, KW), f_map),
                ANY,
            ],
            out_specs=pl.BlockSpec((CHIPS, 32, KV), lambda i, *_: (0, 0, 0)),
            scratch_shapes=[
                pltpu.VMEM((KEYS, KW), BF),
                pltpu.VMEM((QROWS, KEYS), F32),
                pltpu.VMEM((QROWS, 128), F32),
                pltpu.VMEM((QROWS, 128), F32),
                pltpu.VMEM((QROWS, KV), F32),
                pltpu.SemaphoreType.DMA((MAXP,)),
            ],
        ),
        compiler_params=params(),
    )(ids, migration, table, lengths, queries, fresh, cache)


def value_body(ids, mig, kept, moved, w_own, w_sib, o_ref, x_ref):
    grp, core = ids[0], ids[3]
    for k in range(CHIPS):
        first = mig[(2 * k + core) * 4 + grp] == 0
        a, b = kept[k], moved[(k + CHIPS // 2) % CHIPS]
        x_ref[k * 64 : k * 64 + 32, :] = jnp.where(first, b, a)
        x_ref[k * 64 + 32 : k * 64 + 64, :] = jnp.where(first, a, b)
    w = jnp.concatenate([w_own[h] for h in range(4)] + [w_sib[h] for h in range(4)], axis=1)
    head = lax.broadcasted_iota(jnp.int32, (256, 1024), 0) % 8
    place = lax.broadcasted_iota(jnp.int32, (256, 1024), 1) // 128
    meant = head == (place + 4 * core) % 8
    pick = lax.broadcasted_iota(jnp.int32, (32, 256), 1) // 8
    pick = (pick == lax.broadcasted_iota(jnp.int32, (32, 256), 0)).astype(BF)
    for n in range(4):
        y = dot(x_ref[n * 256 : (n + 1) * 256, :], w)
        y = jnp.where(meant, y, 0.0).astype(BF)
        o_ref[n * 32 : (n + 1) * 32, :] = dot(pick, y).astype(BF)


def value(ids, migration, kept, moved, w_own, w_sib):
    return pl.pallas_call(
        value_body,
        out_shape=shape((128, 1024)),
        in_specs=[SMEM, SMEM, VMEM, VMEM, VMEM, VMEM],
        out_specs=VMEM,
        scratch_shapes=[pltpu.VMEM((1024, KV), BF)],
        compiler_params=params(),
    )(ids, migration, kept, moved, w_own, w_sib)


def mix_body(ids, h0, h1, h2, h3, w_own, w_sib, o_ref, h_ref):
    @pl.when(pl.program_id(0) == 0)
    def _():
        for s, h in enumerate((h0, h1, h2, h3)):
            h_ref[(ids[0] - s) & 3] = h[...]

    h = h_ref[...].reshape(512, 1024)
    out = dot(h[:, :512], w_own[...]) + dot(h[:, 512:], w_sib[...])
    for k in range(CHIPS):
        parts = [out[y * 128 + k * 8 : y * 128 + k * 8 + 8] for y in range(4)]
        o_ref[k] = jnp.concatenate(parts, axis=0).astype(BF)


def mix(ids, hs, w_own, w_sib):
    col = 256
    h_spec = pl.BlockSpec((128, 1024), lambda i, ids: (0, 0))
    w_spec = pl.BlockSpec((512, col), lambda i, ids: (0, i))
    return pl.pallas_call(
        mix_body,
        out_shape=shape((CHIPS, 32, DCOL)),
        grid_spec=pltpu.PrefetchScalarGridSpec(
            num_scalar_prefetch=1,
            grid=(DCOL // col,),
            in_specs=[h_spec] * 4 + [w_spec] * 2,
            out_specs=pl.BlockSpec((CHIPS, 32, col), lambda i, ids: (0, 0, i)),
            scratch_shapes=[pltpu.VMEM((4, 128, 1024), BF)],
        ),
        compiler_params=params(),
    )(ids, *hs, w_own, w_sib)


def norm_body(r_ref, res, gain, m_ref, a_ref, b_ref):
    mixed = res[...].astype(F32)
    for k in range(CHIPS):
        mixed = mixed + r_ref[k].astype(F32)
    m_ref[...] = mixed
    scaled = (mixed * gain[...].astype(F32)).astype(BF)
    a_ref[...] = scaled[:, :HALF]
    b_ref[:, :HALF] = scaled[:, HALF:]
    square = jnp.sum(mixed * mixed, axis=1, keepdims=True)
    high = square.astype(BF)
    low = (square - high.astype(F32)).astype(BF)
    lane = lax.broadcasted_iota(jnp.int32, (32, 128), 1)
    b_ref[:, HALF:] = jnp.where(lane < 64, high.astype(F32), low.astype(F32)).astype(BF)


def norm(received, residual, gain):
    return pl.pallas_call(
        norm_body,
        out_shape=(shape((32, DCOL), F32), shape((32, HALF)), shape((32, HALF + 128))),
        in_specs=[VMEM] * 3,
        out_specs=(VMEM,) * 3,
        compiler_params=params(),
    )(received, residual, gain)


def lay_body(a0, a1, a2, a3, b0, b1, b2, b3, a_ref, b_ref):
    for s, a in enumerate((a0, a1, a2, a3)):
        a_ref[-s % 4] = a[...]
    for s, b in enumerate((b0, b1, b2, b3)):
        b_ref[-s % 4] = b[...]


def lay(a, b):
    return pl.pallas_call(
        lay_body,
        out_shape=(shape((4, 32, HALF)), shape((4, 32, HALF + 128))),
        in_specs=[VMEM] * 8,
        out_specs=(VMEM,) * 2,
        compiler_params=params(),
    )(*a, *b)


def gate_up_body(ids, a0, a1, a2, a3, b0, b1, b2, b3, g_own, g_sib, u_own, u_sib, o0, o1, o2, o3, x_ref, w_ref, sems):
    copies = []
    for n, w in enumerate((g_own, g_sib, u_own, u_sib)):
        copy = pltpu.make_async_copy(w, w_ref.at[n], sems.at[n])
        copy.start()
        copies.append(copy)
    grp = ids[0]
    outs = (o0, o1, o2, o3)
    for s, a in enumerate((a0, a1, a2, a3)):
        x_ref[(-s - grp) & 3, :, :HALF] = a[...].reshape(128, HALF)
    for dz in range(4):
        for s, b in enumerate((b0, b1, b2, b3)):
            dx = -s % 4
            x_ref[(dz - grp) & 3, dx * 32 : dx * 32 + 32, HALF:] = b[dz]
    x = x_ref[:, :, :DCOL].reshape(512, DCOL)
    for s in range(4):
        outs[s][:, 2 * FFW :] = x_ref[s, :, DCOL:]
    for n in range(2):
        copies[2 * n].wait()
        own = dot(x, w_ref[2 * n])
        copies[2 * n + 1].wait()
        sib = dot(x, w_ref[2 * n + 1])
        rest = jnp.concatenate([own[:, 512:], sib[:, 512:]], axis=1)
        for s in range(4):
            rows = slice(s * 128, s * 128 + 128)
            base = n * FFW
            outs[s][:, base : base + 512] = own[rows, :512].astype(BF)
            outs[s][:, base + 512 : base + 1024] = sib[rows, :512].astype(BF)
            outs[s][:, base + 1024 : base + FFW] = rest[rows].astype(BF)


def gate_up(ids, a, b, weights):
    return pl.pallas_call(
        gate_up_body,
        out_shape=(shape((128, GW)),) * 4,
        in_specs=[SMEM] + [VMEM] * 8 + [ANY] * 4,
        out_specs=(VMEM,) * 4,
        scratch_shapes=[
            pltpu.VMEM((4, 128, DCOL + 128), BF),
            pltpu.VMEM((4, DCOL, 576), BF),
            pltpu.SemaphoreType.DMA((4,)),
        ],
        compiler_params=params(),
    )(ids, *a, *b, *weights)


def hidden_body(g0, g1, g2, g3, o_ref):
    total = g0[...].astype(F32) + g1[...].astype(F32) + g2[...].astype(F32) + g3[...].astype(F32)
    square = jnp.sum(total[:, 2 * FFW :], axis=1, keepdims=True) * (1.0 / 64)
    scale = lax.rsqrt(square / D + tiny_eps)
    gate = total[:, :FFW] * scale
    up = total[:, FFW : 2 * FFW] * scale
    o_ref[...] = (gate / (1.0 + jnp.exp(-gate)) * up).astype(BF)


def hidden_of(parts):
    return pl.pallas_call(
        hidden_body,
        out_shape=shape((128, FFW)),
        in_specs=[VMEM] * 4,
        out_specs=VMEM,
        compiler_params=params(),
    )(*parts)


def down_body(ids, h0, h1, h2, h3, w_own, w_sib, o_ref, h_ref):
    @pl.when(pl.program_id(0) == 0)
    def _():
        for s, h in enumerate((h0, h1, h2, h3)):
            h_ref[(ids[0] - s) & 3] = h[...]

    h = h_ref[...].reshape(512, FFW)
    rest = jnp.concatenate([w_own[512:, :], w_sib[512:, :]], axis=0)
    out = dot(h[:, :512], w_own[:512, :]) + dot(h[:, 512:1024], w_sib[:512, :]) + dot(h[:, 1024:], rest)
    for dz in range(4):
        for dx in range(4):
            k = ((ids[1] + dz) & 3) * 4 + ((ids[2] + dx) & 3)
            first = (dz * 4 + dx) * 32
            o_ref[k] = out[first : first + 32].astype(BF)


def down(ids, hs, w_own, w_sib):
    col = 256
    h_spec = pl.BlockSpec((128, FFW), lambda i, ids: (0, 0))
    w_spec = pl.BlockSpec((576, col), lambda i, ids: (0, i))
    return pl.pallas_call(
        down_body,
        out_shape=shape((CHIPS, 32, DCOL)),
        grid_spec=pltpu.PrefetchScalarGridSpec(
            num_scalar_prefetch=1,
            grid=(DCOL // col,),
            in_specs=[h_spec] * 4 + [w_spec] * 2,
            out_specs=pl.BlockSpec((CHIPS, 32, col), lambda i, ids: (0, 0, i)),
            scratch_shapes=[pltpu.VMEM((4, 128, FFW), BF)],
        ),
        compiler_params=params(),
    )(ids, *hs, w_own, w_sib)


def finish_body(r_ref, m_ref, o_ref):
    total = m_ref[...]
    for k in range(CHIPS):
        total = total + r_ref[k].astype(F32)
    o_ref[...] = total.astype(BF)


def finish(received, mixed):
    return pl.pallas_call(
        finish_body,
        out_shape=shape((32, DCOL)),
        in_specs=[VMEM] * 2,
        out_specs=VMEM,
        compiler_params=params(),
    )(received, mixed)


def route(dz, dx, flip):
    pairs = []
    for z in range(4):
        for x in range(4):
            for core in range(2):
                to = (z + dz) % 4 * 8 + (x + dx) % 4 * 2 + (core ^ flip)
                pairs.append((z * 8 + x * 2 + core, to))
    return pairs


def sent(block, dz=0, dx=0, flip=0):
    return lax.ppermute(block, "dp", route(dz, dx, flip))


def turned(block, s):
    return lax.ppermute(block, "grp", [(i, (i + s) % 4) for i in range(4)])


def traded(blocks):
    same_core = [list(range(core, 32, 2)) for core in range(2)]
    return lax.all_to_all(blocks, "dp", 0, 0, tiled=True, axis_index_groups=same_core)


def on_device(
    queries,
    new_latent,
    latent_cache,
    block_table,
    lengths,
    migration,
    residual,
    value_projection_weight,
    output_proj,
    norm_gain,
    gate_proj,
    up_proj,
    down_projection_matrix,
):
    dp = lax.axis_index("dp")
    grp = lax.axis_index("grp")
    ids = jnp.stack([grp, dp // 8, dp // 2 % 4, dp % 2, dp * 4 + grp, grp, grp, grp]).astype(jnp.int32)
    queries = queries.reshape(2, QROWS, KW)
    fresh = jnp.pad(new_latent, ((0, 0), (0, 16 - STEPS), (0, 0)))
    residual_rows = residual.reshape(32, DCOL)
    gain = norm_gain.reshape(1, DCOL)

    outgoing = pack(ids, migration, queries, fresh)
    arrived = sent(outgoing, dz=2)
    value_sib = sent(value_projection_weight, flip=1)
    out_sib = sent(output_proj, flip=1)
    gate_sib = sent(gate_proj, flip=1)
    up_sib = sent(up_proj, flip=1)
    down_sib = sent(down_projection_matrix, flip=1)

    kept = attend(False, ids, migration, block_table, lengths, queries, fresh, latent_cache)
    moved = attend(True, ids, migration, block_table, lengths, arrived, arrived, latent_cache)
    kept = traded(kept)
    moved = traded(moved)
    heads = value(ids, migration, kept, moved, value_projection_weight, value_sib)
    heads = [heads] + [turned(heads, s) for s in (1, 2, 3)]
    partial = mix(ids, heads, output_proj, out_sib)
    mixed, a, b = norm(traded(partial), residual_rows, gain)
    a, b = lay(
        [a] + [sent(a, dx=s) for s in (1, 2, 3)],
        [b] + [sent(b, dz=s) for s in (1, 2, 3)],
    )
    parts = gate_up(
        ids,
        [a] + [sent(a, dz=s) for s in (1, 2, 3)],
        [b] + [sent(b, dx=s) for s in (1, 2, 3)],
        (gate_proj, gate_sib, up_proj, up_sib),
    )
    hid = hidden_of([parts[0]] + [turned(parts[s], s) for s in (1, 2, 3)])
    hid = [hid] + [turned(hid, s) for s in (1, 2, 3)]
    partial = down(ids, hid, down_projection_matrix, down_sib)
    out = finish(traded(partial), mixed)
    return out.reshape(8, 4, DCOL)


def solution(mesh):
    placed = (
        P(("dp", "grp"), None, None, None),
        P(("dp", "grp"), None, None),
        P(("dp", "grp"), None, None),
        P(("dp", "grp"), None),
        P(),
        P(),
        P("dp", None, "grp"),
        P("dp", None, None),
        P("dp", "grp"),
        P("grp"),
        P("grp", "dp"),
        P("grp", "dp"),
        P("dp", "grp"),
    )
    return jax.shard_map(
        on_device, mesh=mesh, in_specs=placed, out_specs=P("dp", None, "grp"), check_vma=False
    )
```

```python
import functools

import jax
import jax.numpy as jnp
from jax import lax
from jax.experimental import pallas as pl
from jax.experimental.pallas import tpu as pltpu
from jax.sharding import PartitionSpec as P

D = 7168
KV = 512
KW = 576
PAGE = 64
MAXP = 32
STEPS = 4
HEADS = 128
TOKENS = PAGE * MAXP
BLOCK = 256
CHUNK = 512
KEYS = TOKENS + 128
QROWS = STEPS * HEADS
CHIPS = 16
DCOL = D // 4
FFW = 1152
GW = 2 * FFW + 128

score_scale = 0.07216878364870323
exp2_scale = score_scale * 1.4426950408889634
tiny_eps = 1e-06
neg_fill = -1e30

BF = jnp.bfloat16
F32 = jnp.float32
VMEM = pl.BlockSpec(memory_space=pltpu.VMEM)
SMEM = pl.BlockSpec(memory_space=pltpu.SMEM)
ANY = pl.BlockSpec(memory_space=pl.ANY)
HBM = pl.BlockSpec(memory_space=pltpu.HBM)


def params(mb=48):
    return pltpu.CompilerParams(vmem_limit_bytes=mb * 1024 * 1024)


def shape(dims, kind=BF):
    return jax.ShapeDtypeStruct(dims, kind)


def dot(a, b):
    return jnp.dot(a, b, preferred_element_type=F32)


def dot_t(a, b):
    return lax.dot_general(a, b, (((1,), (1,)), ((), ())), preferred_element_type=F32)


def pack_body(ids, mig, q_ref, f_ref, qo_ref, fo_ref, sems):
    one = pl.ds(mig[ids[4]], 1)
    copies = [copy_of(q_ref.at[one], qo_ref, sems.at[0]), copy_of(f_ref.at[one], fo_ref, sems.at[1])]
    start(copies)
    finished(copies)


def pack(ids, migration, queries, fresh):
    return pl.pallas_call(
        pack_body,
        out_shape=(shape((1, STEPS, KW, HEADS)), shape((1, STEPS, KW))),
        in_specs=[SMEM, SMEM, HBM, HBM],
        out_specs=(HBM, HBM),
        scratch_shapes=[pltpu.SemaphoreType.DMA((2,))],
        compiler_params=params(),
    )(ids, migration, queries, fresh)


def copy_of(source, target, sem):
    return pltpu.make_async_copy(source, target, sem)


def start(copies):
    for copy in copies:
        copy.start()


def finished(copies):
    for copy in copies:
        copy.wait()


def attend_body(moved, ids, mig, table, lengths, q_ref, f_ref, cache, *refs):
    o_ref, kbuf, q_buf, sems = refs[-4:]
    own = mig[ids[4]]
    row = own if moved else 1 - own
    length = lengths[ids[4] * 2 + row]
    per = CHUNK // PAGE
    groups = [
        [
            copy_of(cache.at[table[row, i]], kbuf.at[pl.ds(i * PAGE, PAGE), :], sems.at[i])
            for i in range(c * per, (c + 1) * per)
        ]
        for c in range(TOKENS // CHUNK)
    ]
    start(groups[0])
    start(groups[1])
    eye = lax.broadcasted_iota(jnp.int32, (HEADS, HEADS), 0)
    eye = (eye == lax.broadcasted_iota(jnp.int32, (HEADS, HEADS), 1)).astype(BF)
    for t in range(STEPS):
        q_buf[t * HEADS : (t + 1) * HEADS, :] = dot_t(eye, q_ref[0, t]).astype(BF)
    kbuf[TOKENS : TOKENS + 16, :] = f_ref[0]
    kbuf[TOKENS + 16 :, :] = jnp.zeros((KEYS - TOKENS - 16, KW), BF)
    key = lax.broadcasted_iota(jnp.int32, (8, TOKENS), 1)
    past = jnp.where(key < length, 0.0, neg_fill)[0:1]
    place = lax.broadcasted_iota(jnp.int32, (BLOCK, 128), 1)
    step = lax.broadcasted_iota(jnp.int32, (BLOCK, 128), 0) // HEADS
    blocks = []
    for n in range(QROWS // BLOCK):
        q = q_buf[n * BLOCK : (n + 1) * BLOCK, :]
        fresh = dot_t(q, kbuf[TOKENS:, :])
        scores = [jnp.where(place <= step + n * (BLOCK // HEADS), fresh, neg_fill)]
        for c, group in enumerate(groups):
            if n == 0:
                finished(group)
                if c + 2 < len(groups):
                    start(groups[c + 2])
            keys = slice(c * CHUNK, (c + 1) * CHUNK)
            scores.append(dot_t(q, kbuf[keys, :]) + past[:, keys])
        blocks.append(scores)
    for n, scores in enumerate(blocks):
        top = functools.reduce(jnp.maximum, [jnp.max(s, axis=1, keepdims=True) for s in scores])
        weights = [jnp.exp2((s - top) * exp2_scale) for s in scores]
        total = functools.reduce(jnp.add, [jnp.sum(w, axis=1, keepdims=True) for w in weights])
        weight = jnp.concatenate([w.astype(BF) for w in weights[1:] + weights[:1]], axis=1)
        out = dot(weight, kbuf[:, :KV]) / total
        for k in range(CHIPS):
            parts = [out[t * HEADS + k * 8 : t * HEADS + k * 8 + 8] for t in range(BLOCK // HEADS)]
            o_ref[k, n * 16 : n * 16 + 16, :] = jnp.concatenate(parts, axis=0).astype(BF)


def attend(moved, ids, migration, table, lengths, queries, fresh, cache, after):
    if moved:
        q_map = lambda i, ids, mig, tab, lens: (0, 0, 0, 0)
        f_map = lambda i, ids, mig, tab, lens: (0, 0, 0)
    else:
        q_map = lambda i, ids, mig, tab, lens: (1 - mig[ids[4]], 0, 0, 0)
        f_map = lambda i, ids, mig, tab, lens: (1 - mig[ids[4]], 0, 0)
    return pl.pallas_call(
        functools.partial(attend_body, moved),
        out_shape=shape((CHIPS, 32, KV)),
        grid_spec=pltpu.PrefetchScalarGridSpec(
            num_scalar_prefetch=4,
            grid=(1,),
            in_specs=[
                pl.BlockSpec((1, STEPS, KW, HEADS), q_map),
                pl.BlockSpec((1, 16, KW), f_map),
                HBM,
            ]
            + [ANY] * len(after),
            out_specs=pl.BlockSpec((CHIPS, 32, KV), lambda i, *_: (0, 0, 0)),
            scratch_shapes=[
                pltpu.VMEM((KEYS, KW), BF),
                pltpu.VMEM((QROWS, KW), BF),
                pltpu.SemaphoreType.DMA((MAXP,)),
            ],
        ),
        compiler_params=params(),
    )(ids, migration, table, lengths, queries, fresh, cache, *after)


def value_body(moved, ids, r_ref, w_own, w_sib, _, o_ref):
    core = ids[3]
    half = CHIPS // 2
    w = jnp.concatenate([w_own[h] for h in range(4)] + [w_sib[h] for h in range(4)], axis=1)
    head = lax.broadcasted_iota(jnp.int32, (256, 1024), 0) % 8
    place = lax.broadcasted_iota(jnp.int32, (256, 1024), 1) // 128
    meant = head == (place + 4 * core) % 8
    pick = lax.broadcasted_iota(jnp.int32, (32, 256), 1) // 8
    pick = (pick == lax.broadcasted_iota(jnp.int32, (32, 256), 0)).astype(BF)
    for n in range(2):
        at = (1 - n if moved else n) * half
        y = dot(r_ref[at : at + half].reshape(256, KV), w)
        y = jnp.where(meant, y, 0.0).astype(BF)
        o_ref[n * 32 : (n + 1) * 32, :] = dot(pick, y).astype(BF)


def value(moved, ids, received, w_own, w_sib, after):
    return pl.pallas_call(
        functools.partial(value_body, moved),
        out_shape=shape((64, 1024)),
        in_specs=[SMEM, VMEM, VMEM, VMEM, ANY],
        out_specs=VMEM,
        compiler_params=params(),
    )(ids, received, w_own, w_sib, after)


SPANS = ((0, 768), (768, 1792))


def column_copies(w_own, w_sib, w_ref, sems, depth):
    groups = []
    for n, (at, end) in enumerate(SPANS):
        cols = pl.ds(at, end - at)
        groups.append(
            [
                copy_of(w.at[:, cols], w_ref.at[pl.ds(i * depth, depth), cols], sems.at[n, i])
                for i, w in enumerate((w_own, w_sib))
            ]
        )
        start(groups[-1])
    return groups


def mix_body(ids, k0, k1, k2, k3, m0, m1, m2, m3, w_own, w_sib, o_ref, h_ref, p_ref, w_ref, sems):
    groups = column_copies(w_own, w_sib, w_ref, sems, 512)
    to = lax.broadcasted_iota(jnp.int32, (256, 256), 0)
    of = lax.broadcasted_iota(jnp.int32, (256, 256), 1)
    order = ((to // 4 % 4) * 64 + (to // 16) * 4 + to % 4 == of).astype(BF)
    for n, hs in enumerate(((k0, k1, k2, k3), (m0, m1, m2, m3))):
        for s, h in enumerate(hs):
            h_ref[(ids[0] - s) & 3] = h[...]
        p_ref[n * 256 : (n + 1) * 256, :] = dot(order, h_ref[...].reshape(256, 1024)).astype(BF)
    for n, (at, end) in enumerate(SPANS):
        finished(groups[n])
        out = dot(p_ref[...], w_ref[:, at:end]).astype(BF)
        o_ref[:, :16, at:end] = out[:256].reshape(CHIPS, 16, end - at)
        o_ref[:, 16:, at:end] = out[256:].reshape(CHIPS, 16, end - at)


def mix(ids, kept, moved, w_own, w_sib):
    return pl.pallas_call(
        mix_body,
        out_shape=shape((CHIPS, 32, DCOL)),
        in_specs=[SMEM] + [VMEM] * 8 + [HBM] * 2,
        out_specs=VMEM,
        scratch_shapes=[
            pltpu.VMEM((4, 64, 1024), BF),
            pltpu.VMEM((512, 1024), BF),
            pltpu.VMEM((1024, DCOL), BF),
            pltpu.SemaphoreType.DMA((2, 2)),
        ],
        compiler_params=params(),
    )(ids, *kept, *moved, w_own, w_sib)


def norm_body(r_ref, res, gain, m_ref, o_ref):
    mixed = res[...].astype(F32)
    for k in range(CHIPS):
        mixed = mixed + r_ref[k].astype(F32)
    m_ref[...] = mixed
    scaled = (mixed * gain[...].astype(F32)).astype(BF)
    square = jnp.sum(mixed * mixed, axis=1, keepdims=True)
    high = square.astype(BF).astype(F32)
    lane = lax.broadcasted_iota(jnp.int32, (32, 128), 1)
    square = jnp.where(lane < 64, high, square - high).astype(BF)
    for k in range(CHIPS):
        o_ref[k, :, :DCOL] = scaled
        o_ref[k, :, DCOL:] = square


def norm(received, residual, gain):
    return pl.pallas_call(
        norm_body,
        out_shape=(shape((32, DCOL), F32), shape((CHIPS, 32, DCOL + 128))),
        in_specs=[VMEM] * 3,
        out_specs=(VMEM,) * 2,
        compiler_params=params(),
    )(received, residual, gain)


PIECES = ((0, 0, 128), (1, 0, 64), (1, 64, 128), (2, 0, 64), (2, 64, 128), (3, 0, 64), (3, 64, 128))


def gate_up_body(ids, x_in, g_own, g_sib, u_own, u_sib, *refs):
    outs, (x_ref, w_ref, sems) = refs[: len(PIECES)], refs[len(PIECES) :]
    groups = []
    for n in range(2 * FFW // 768):
        group = []
        at, end = n * 768, (n + 1) * 768
        while at < end:
            which, row = divmod(at, 576)
            count = min(end - at, 576 - row)
            source = (g_own, g_sib, u_own, u_sib)[which].at[pl.ds(row, count), :]
            group.append(copy_of(source, w_ref.at[pl.ds(at, count), :], sems.at[n, len(group)]))
            at += count
        start(group)
        groups.append(group)
    for s in range(4):
        first = ((ids[0] + s) & 3) * 4
        for i in range(4):
            x_ref[s * 128 + i * 32 : s * 128 + i * 32 + 32, :] = x_in[first + i]
    for n in range(2 * FFW // 768):
        finished(groups[n])
        cols = slice(n * 768, (n + 1) * 768)
        out = dot_t(x_ref[:, :DCOL], w_ref[cols, :]).astype(BF)
        for piece, (s, top, end) in zip(outs, PIECES):
            piece[:, cols] = out[s * 128 + top : s * 128 + end]
    for piece, (s, top, end) in zip(outs, PIECES):
        piece[:, 2 * FFW :] = x_ref[s * 128 + top : s * 128 + end, DCOL:]


def gate_up(ids, x, weights):
    return pl.pallas_call(
        gate_up_body,
        out_shape=tuple(shape((end - top, GW)) for _, top, end in PIECES),
        in_specs=[SMEM, VMEM] + [HBM] * 4,
        out_specs=(VMEM,) * len(PIECES),
        scratch_shapes=[
            pltpu.VMEM((512, DCOL + 128), BF),
            pltpu.VMEM((2 * FFW, DCOL), BF),
            pltpu.SemaphoreType.DMA((2 * FFW // 768, 2)),
        ],
        compiler_params=params(),
    )(ids, x, *weights)


def pass_body(a, b, c, d, o_ref, p_ref):
    o_ref[...] = (a[...].astype(F32) + b[...].astype(F32)).astype(BF)
    p_ref[...] = (c[...].astype(F32) + d[...].astype(F32)).astype(BF)


def pass_on(a, b, c, d):
    return pl.pallas_call(
        pass_body,
        out_shape=(shape((64, GW)),) * 2,
        in_specs=[VMEM] * 4,
        out_specs=(VMEM,) * 2,
        compiler_params=params(),
    )(a, b, c, d)


def hidden_body(own, a_low, a_high, b_low, b_high, o_ref):
    for n, (a, b) in enumerate(((a_low, b_low), (a_high, b_high))):
        rows = slice(n * 64, n * 64 + 64)
        total = own[rows, :].astype(F32) + a[...].astype(F32) + b[...].astype(F32)
        square = jnp.sum(total[:, 2 * FFW :], axis=1, keepdims=True) * (1.0 / 64)
        scale = lax.rsqrt(square / D + tiny_eps)
        gate = total[:, :FFW] * scale
        up = total[:, FFW : 2 * FFW] * scale
        o_ref[rows, :] = (gate / (1.0 + jnp.exp(-gate)) * up).astype(BF)


def hidden_of(*parts):
    return pl.pallas_call(
        hidden_body,
        out_shape=shape((128, FFW)),
        in_specs=[VMEM] * 5,
        out_specs=VMEM,
        compiler_params=params(),
    )(*parts)


def down_body(ids, h0, h1, h2, h3, w_own, w_sib, o_ref, h_ref, w_ref, sems):
    groups = column_copies(w_own, w_sib, w_ref, sems, 576)
    for s, h in enumerate((h0, h1, h2, h3)):
        h_ref[(ids[0] - s) & 3] = h[...]
    for n, (at, end) in enumerate(SPANS):
        finished(groups[n])
        out = dot(h_ref[...].reshape(512, FFW), w_ref[:, at:end]).astype(BF)
        o_ref[:, :, at:end] = out.reshape(CHIPS, 32, end - at)


def down(ids, hs, w_own, w_sib):
    return pl.pallas_call(
        down_body,
        out_shape=shape((CHIPS, 32, DCOL)),
        in_specs=[SMEM] + [VMEM] * 4 + [HBM] * 2,
        out_specs=VMEM,
        scratch_shapes=[
            pltpu.VMEM((4, 128, FFW), BF),
            pltpu.VMEM((FFW, DCOL), BF),
            pltpu.SemaphoreType.DMA((2, 2)),
        ],
        compiler_params=params(),
    )(ids, *hs, w_own, w_sib)


def finish_body(r_ref, m_ref, o_ref):
    total = m_ref[...]
    for k in range(CHIPS):
        total = total + r_ref[k].astype(F32)
    o_ref[...] = total.astype(BF)


def finish(received, mixed):
    return pl.pallas_call(
        finish_body,
        out_shape=shape((32, DCOL)),
        in_specs=[VMEM] * 2,
        out_specs=VMEM,
        compiler_params=params(),
    )(received, mixed)


def route(dz, dx, flip):
    pairs = []
    for z in range(4):
        for x in range(4):
            for core in range(2):
                to = (z + dz) % 4 * 8 + (x + dx) % 4 * 2 + (core ^ flip)
                pairs.append((z * 8 + x * 2 + core, to))
    return pairs


def sent(block, dz=0, dx=0, flip=0):
    return lax.ppermute(block, "dp", route(dz, dx, flip))


def turned(block, s):
    return lax.ppermute(block, "grp", [(i, (i + s) % 4) for i in range(4)])


def traded(blocks):
    same_core = [list(range(core, 32, 2)) for core in range(2)]
    return lax.all_to_all(blocks, "dp", 0, 0, tiled=True, axis_index_groups=same_core)


def padded(fresh):
    return jnp.pad(fresh, ((0, 0), (0, 16 - STEPS), (0, 0)))


def on_device(
    queries,
    new_latent,
    latent_cache,
    block_table,
    lengths,
    migration,
    residual,
    value_projection_weight,
    output_proj,
    norm_gain,
    gate_proj,
    up_proj,
    down_projection_matrix,
):
    dp = lax.axis_index("dp")
    grp = lax.axis_index("grp")
    ids = jnp.stack([grp, dp // 8, dp // 2 % 4, dp % 2, dp * 4 + grp, grp, grp, grp]).astype(jnp.int32)
    queries = queries.reshape(2, STEPS, HEADS, KW).transpose(0, 1, 3, 2)
    fresh = padded(new_latent)
    gain = norm_gain.reshape(1, DCOL)
    places = lax.dynamic_slice_in_dim(migration, dp * 4, 4)
    places = places.reshape(4, 1, 1)
    rows = residual.reshape(4, 2, STEPS, DCOL)
    low, high = rows[:, 0], rows[:, 1]
    rows = jnp.stack([jnp.where(places == 0, high, low), jnp.where(places == 0, low, high)])
    rows = rows.reshape(32, DCOL)

    q_out, f_out = pack(ids, migration, queries, new_latent)
    q_in, f_in = sent(q_out, dz=2), padded(sent(f_out, dz=2))
    value_sib = sent(value_projection_weight, flip=1)
    out_sib = sent(output_proj, flip=1)
    gate, up = gate_proj.T, up_proj.T
    gate_sib = sent(gate, flip=1)
    up_sib = sent(up, flip=1)
    down_sib = sent(down_projection_matrix, flip=1)

    def attention(moved, queries, fresh, after):
        return attend(moved, ids, migration, block_table, lengths, queries, fresh, latent_cache, after)

    def project(moved, latent, after):
        return value(moved, ids, latent, value_projection_weight, value_sib, after)

    def spread(block):
        return [block] + [turned(block, s) for s in (1, 2, 3)]

    k_lat = attention(False, queries, fresh, [])
    k_lat_in = traded(k_lat)
    m_lat = attention(True, q_in, f_in, [k_lat, value_sib, out_sib, gate_sib, up_sib, down_sib])
    m_lat_in = traded(m_lat)
    k_heads = project(False, k_lat_in, m_lat)
    m_heads = project(True, m_lat_in, k_heads)
    partial = mix(ids, spread(k_heads), spread(m_heads), output_proj, out_sib)
    mixed, scaled = norm(traded(partial), rows, gain)
    own, a_low, a_high, c_low, c_high, b_low, b_high = gate_up(
        ids, traded(scaled), (gate, gate_sib, up, up_sib)
    )
    c_low, c_high = turned(c_low, 1), turned(c_high, 3)
    a_high, b_low = turned(a_high, 1), turned(b_low, 3)
    a_low, b_high = pass_on(a_low, c_low, b_high, c_high)
    a_low, b_high = turned(a_low, 1), turned(b_high, 3)
    hid = spread(hidden_of(own, a_low, a_high, b_low, b_high))
    partial = down(ids, hid, down_projection_matrix, down_sib)
    out = finish(traded(partial), mixed).reshape(2, 4, STEPS, DCOL)
    out = jnp.stack([jnp.where(places == j, out[1], out[0]) for j in range(2)], axis=1)
    return out.reshape(8, STEPS, DCOL)


def solution(mesh):
    placed = (
        P(("dp", "grp"), None, None, None),
        P(("dp", "grp"), None, None),
        P(("dp", "grp"), None, None),
        P(("dp", "grp"), None),
        P(),
        P(),
        P("dp", None, "grp"),
        P("dp", None, None),
        P("dp", "grp"),
        P("grp"),
        P("grp", "dp"),
        P("grp", "dp"),
        P("dp", "grp"),
    )
    return jax.shard_map(
        on_device, mesh=mesh, in_specs=placed, out_specs=P("dp", None, "grp"), check_vma=False
    )
```

```python
import functools

import jax
import jax.numpy as jnp
from jax import lax
from jax.experimental import pallas as pl
from jax.experimental.pallas import tpu as pltpu
from jax.sharding import PartitionSpec as P

D = 7168
KV = 512
KW = 576
PAGE = 64
MAXP = 32
STEPS = 4
HEADS = 128
TOKENS = PAGE * MAXP
BLOCK = 256
CHUNK = 512
KEYS = TOKENS + 128
QROWS = STEPS * HEADS
TROWS = STEPS * KW
FROWS = 5 * 16
CHIPS = 16
DCOL = D // 4
FFW = 1152
GW = 2 * FFW + 128

score_scale = 0.07216878364870323
exp2_scale = score_scale * 1.4426950408889634
tiny_eps = 1e-06
neg_fill = -1e30

BF = jnp.bfloat16
F32 = jnp.float32
VMEM = pl.BlockSpec(memory_space=pltpu.VMEM)
SMEM = pl.BlockSpec(memory_space=pltpu.SMEM)
ANY = pl.BlockSpec(memory_space=pl.ANY)
HBM = pl.BlockSpec(memory_space=pltpu.HBM)


def params(mb=48):
    return pltpu.CompilerParams(vmem_limit_bytes=mb * 1024 * 1024)


def shape(dims, kind=BF):
    return jax.ShapeDtypeStruct(dims, kind)


def dot(a, b):
    return jnp.dot(a, b, preferred_element_type=F32)


def dot_t(a, b):
    return lax.dot_general(a, b, (((1,), (1,)), ((), ())), preferred_element_type=F32)


def pack_body(ids, mig, q_ref, f_ref, o_ref):
    o_ref[0, :TROWS, :] = q_ref[0]
    o_ref[0, TROWS:, :] = f_ref[0]


def pack(ids, migration, queries, fresh):
    return pl.pallas_call(
        pack_body,
        out_shape=shape((1, TROWS + FROWS, HEADS)),
        grid_spec=pltpu.PrefetchScalarGridSpec(
            num_scalar_prefetch=2,
            grid=(1,),
            in_specs=[
                pl.BlockSpec((1, TROWS, HEADS), lambda i, ids, mig: (mig[ids[4]], 0, 0)),
                pl.BlockSpec((1, FROWS, HEADS), lambda i, ids, mig: (mig[ids[4]], 0, 0)),
            ],
            out_specs=pl.BlockSpec((1, TROWS + FROWS, HEADS), lambda i, ids, mig: (0, 0, 0)),
        ),
        compiler_params=params(),
    )(ids, migration, queries, fresh)


def copy_of(source, target, sem):
    return pltpu.make_async_copy(source, target, sem)


def start(copies):
    for copy in copies:
        copy.start()


def finished(copies):
    for copy in copies:
        copy.wait()


def attend_body(moved, ids, mig, table, lengths, q_ref, f_ref, cache, *refs):
    o_ref, kbuf, t_buf, f_buf, q_buf, sems, i_sems = refs[-7:]
    own = mig[ids[4]]
    row = own if moved else 1 - own
    slot = 0 if moved else row
    inputs = [
        copy_of(q_ref.at[slot, pl.ds(0, TROWS), :], t_buf, i_sems.at[0]),
        copy_of(f_ref.at[slot, pl.ds(TROWS if moved else 0, FROWS), :], f_buf, i_sems.at[1]),
    ]
    start(inputs)
    length = lengths[ids[4] * 2 + row]
    per = CHUNK // PAGE
    groups = [
        [
            copy_of(cache.at[table[row, i]], kbuf.at[pl.ds(i * PAGE, PAGE), :], sems.at[i])
            for i in range(c * per, (c + 1) * per)
        ]
        for c in range(TOKENS // CHUNK)
    ]
    start(groups[0])
    start(groups[1])
    eye = lax.broadcasted_iota(jnp.int32, (HEADS, HEADS), 0)
    eye = (eye == lax.broadcasted_iota(jnp.int32, (HEADS, HEADS), 1)).astype(BF)
    kbuf[TOKENS + 16 :, :] = jnp.zeros((KEYS - TOKENS - 16, KW), BF)
    finished(inputs)
    for i in range(5):
        width = min(HEADS, KW - i * HEADS)
        kbuf[TOKENS : TOKENS + 16, i * HEADS : i * HEADS + width] = f_buf[i * 16 : i * 16 + 16, :width]
    for t in range(STEPS):
        q_buf[t * HEADS : (t + 1) * HEADS, :] = dot_t(eye, t_buf[t * KW : (t + 1) * KW, :]).astype(BF)
    key = lax.broadcasted_iota(jnp.int32, (8, TOKENS), 1)
    past = jnp.where(key < length, 0.0, neg_fill)[0:1]
    place = lax.broadcasted_iota(jnp.int32, (BLOCK, 128), 1)
    step = lax.broadcasted_iota(jnp.int32, (BLOCK, 128), 0) // HEADS
    blocks = []
    for n in range(QROWS // BLOCK):
        q = q_buf[n * BLOCK : (n + 1) * BLOCK, :]
        fresh = dot_t(q, kbuf[TOKENS:, :])
        scores = [jnp.where(place <= step + n * (BLOCK // HEADS), fresh, neg_fill)]
        for c, group in enumerate(groups):
            if n == 0:
                finished(group)
                if c + 2 < len(groups):
                    start(groups[c + 2])
            keys = slice(c * CHUNK, (c + 1) * CHUNK)
            scores.append(dot_t(q, kbuf[keys, :]) + past[:, keys])
        blocks.append(scores)
    for n, scores in enumerate(blocks):
        top = functools.reduce(jnp.maximum, [jnp.max(s, axis=1, keepdims=True) for s in scores])
        weights = [jnp.exp2((s - top) * exp2_scale) for s in scores]
        total = functools.reduce(jnp.add, [jnp.sum(w, axis=1, keepdims=True) for w in weights])
        weight = jnp.concatenate([w.astype(BF) for w in weights[1:] + weights[:1]], axis=1)
        out = dot(weight, kbuf[:, :KV]) / total
        for k in range(CHIPS):
            parts = [out[t * HEADS + k * 8 : t * HEADS + k * 8 + 8] for t in range(BLOCK // HEADS)]
            o_ref[k, n * 16 : n * 16 + 16, :] = jnp.concatenate(parts, axis=0).astype(BF)


def attend(moved, ids, migration, table, lengths, queries, fresh, cache, after):
    return pl.pallas_call(
        functools.partial(attend_body, moved),
        out_shape=shape((CHIPS, 32, KV)),
        in_specs=[SMEM] * 4 + [HBM] * 3 + [ANY] * len(after),
        out_specs=VMEM,
        scratch_shapes=[
            pltpu.VMEM((KEYS, KW), BF),
            pltpu.VMEM((TROWS, HEADS), BF),
            pltpu.VMEM((FROWS, HEADS), BF),
            pltpu.VMEM((QROWS, KW), BF),
            pltpu.SemaphoreType.DMA((MAXP,)),
            pltpu.SemaphoreType.DMA((2,)),
        ],
        compiler_params=params(),
    )(ids, migration, table, lengths, queries, fresh, cache, *after)


def value_body(moved, ids, r_ref, w_own, w_sib, *refs):
    o_ref = refs[-1]
    core = ids[3]
    half = CHIPS // 2
    w = jnp.concatenate([w_own[h] for h in range(4)] + [w_sib[h] for h in range(4)], axis=1)
    head = lax.broadcasted_iota(jnp.int32, (256, 1024), 0) % 8
    place = lax.broadcasted_iota(jnp.int32, (256, 1024), 1) // 128
    meant = head == (place + 4 * core) % 8
    pick = lax.broadcasted_iota(jnp.int32, (32, 256), 1) // 8
    pick = (pick == lax.broadcasted_iota(jnp.int32, (32, 256), 0)).astype(BF)
    for n in range(2):
        at = (1 - n if moved else n) * half
        y = dot(r_ref[at : at + half].reshape(256, KV), w)
        y = jnp.where(meant, y, 0.0).astype(BF)
        o_ref[n * 32 : (n + 1) * 32, :] = dot(pick, y).astype(BF)


def value(moved, ids, received, w_own, w_sib, after):
    return pl.pallas_call(
        functools.partial(value_body, moved),
        out_shape=shape((64, 1024)),
        in_specs=[SMEM, VMEM, VMEM, VMEM] + [ANY] * len(after),
        out_specs=VMEM,
        compiler_params=params(),
    )(ids, received, w_own, w_sib, *after)


SPANS = ((0, 768), (768, 1792))


def column_copies(w_own, w_sib, w_ref, sems, depth):
    groups = []
    for n, (at, end) in enumerate(SPANS):
        cols = pl.ds(at, end - at)
        groups.append(
            [
                copy_of(w.at[:, cols], w_ref.at[pl.ds(i * depth, depth), cols], sems.at[n, i])
                for i, w in enumerate((w_own, w_sib))
            ]
        )
        start(groups[-1])
    return groups


def mix_body(ids, k0, k1, k2, k3, m0, m1, m2, m3, w_own, w_sib, o_ref, h_ref, p_ref, w_ref, sems):
    groups = column_copies(w_own, w_sib, w_ref, sems, 512)
    to = lax.broadcasted_iota(jnp.int32, (256, 256), 0)
    of = lax.broadcasted_iota(jnp.int32, (256, 256), 1)
    order = ((to // 4 % 4) * 64 + (to // 16) * 4 + to % 4 == of).astype(BF)
    for n, hs in enumerate(((k0, k1, k2, k3), (m0, m1, m2, m3))):
        for s, h in enumerate(hs):
            h_ref[(ids[0] - s) & 3] = h[...]
        p_ref[n * 256 : (n + 1) * 256, :] = dot(order, h_ref[...].reshape(256, 1024)).astype(BF)
    for n, (at, end) in enumerate(SPANS):
        finished(groups[n])
        out = dot(p_ref[...], w_ref[:, at:end]).astype(BF)
        o_ref[:, :16, at:end] = out[:256].reshape(CHIPS, 16, end - at)
        o_ref[:, 16:, at:end] = out[256:].reshape(CHIPS, 16, end - at)


def mix(ids, kept, moved, w_own, w_sib):
    return pl.pallas_call(
        mix_body,
        out_shape=shape((CHIPS, 32, DCOL)),
        in_specs=[SMEM] + [VMEM] * 8 + [HBM] * 2,
        out_specs=VMEM,
        scratch_shapes=[
            pltpu.VMEM((4, 64, 1024), BF),
            pltpu.VMEM((512, 1024), BF),
            pltpu.VMEM((1024, DCOL), BF),
            pltpu.SemaphoreType.DMA((2, 2)),
        ],
        compiler_params=params(),
    )(ids, *kept, *moved, w_own, w_sib)


def norm_body(r_ref, res, gain, m_ref, o_ref):
    mixed = res[...].astype(F32)
    for k in range(CHIPS):
        mixed = mixed + r_ref[k].astype(F32)
    m_ref[...] = mixed
    scaled = (mixed * gain[...].astype(F32)).astype(BF)
    square = jnp.sum(mixed * mixed, axis=1, keepdims=True)
    high = square.astype(BF).astype(F32)
    lane = lax.broadcasted_iota(jnp.int32, (32, 128), 1)
    square = jnp.where(lane < 64, high, square - high).astype(BF)
    for k in range(CHIPS):
        o_ref[k, :, :DCOL] = scaled
        o_ref[k, :, DCOL:] = square


def norm(received, residual, gain):
    return pl.pallas_call(
        norm_body,
        out_shape=(shape((32, DCOL), F32), shape((CHIPS, 32, DCOL + 128))),
        in_specs=[VMEM] * 3,
        out_specs=(VMEM,) * 2,
        compiler_params=params(),
    )(received, residual, gain)


PIECES = ((0, 0, 128), (1, 0, 64), (1, 64, 128), (2, 0, 64), (2, 64, 128), (3, 0, 64), (3, 64, 128))


def gate_up_body(ids, x_in, g_own, g_sib, u_own, u_sib, *refs):
    outs, (x_ref, w_ref, sems) = refs[: len(PIECES)], refs[len(PIECES) :]
    groups = []
    for n in range(2 * FFW // 768):
        group = []
        at, end = n * 768, (n + 1) * 768
        while at < end:
            which, row = divmod(at, 576)
            count = min(end - at, 576 - row)
            source = (g_own, g_sib, u_own, u_sib)[which].at[pl.ds(row, count), :]
            group.append(copy_of(source, w_ref.at[pl.ds(at, count), :], sems.at[n, len(group)]))
            at += count
        start(group)
        groups.append(group)
    for s in range(4):
        first = ((ids[0] + s) & 3) * 4
        for i in range(4):
            x_ref[s * 128 + i * 32 : s * 128 + i * 32 + 32, :] = x_in[first + i]
    for n in range(2 * FFW // 768):
        finished(groups[n])
        cols = slice(n * 768, (n + 1) * 768)
        out = dot_t(x_ref[:, :DCOL], w_ref[cols, :]).astype(BF)
        for piece, (s, top, end) in zip(outs, PIECES):
            piece[:, cols] = out[s * 128 + top : s * 128 + end]
    for piece, (s, top, end) in zip(outs, PIECES):
        piece[:, 2 * FFW :] = x_ref[s * 128 + top : s * 128 + end, DCOL:]


def gate_up(ids, x, weights):
    return pl.pallas_call(
        gate_up_body,
        out_shape=tuple(shape((end - top, GW)) for _, top, end in PIECES),
        in_specs=[SMEM, VMEM] + [HBM] * 4,
        out_specs=(VMEM,) * len(PIECES),
        scratch_shapes=[
            pltpu.VMEM((512, DCOL + 128), BF),
            pltpu.VMEM((2 * FFW, DCOL), BF),
            pltpu.SemaphoreType.DMA((2 * FFW // 768, 2)),
        ],
        compiler_params=params(),
    )(ids, x, *weights)


def pass_body(a, b, c, d, o_ref, p_ref):
    o_ref[...] = (a[...].astype(F32) + b[...].astype(F32)).astype(BF)
    p_ref[...] = (c[...].astype(F32) + d[...].astype(F32)).astype(BF)


def pass_on(a, b, c, d):
    return pl.pallas_call(
        pass_body,
        out_shape=(shape((64, GW)),) * 2,
        in_specs=[VMEM] * 4,
        out_specs=(VMEM,) * 2,
        compiler_params=params(),
    )(a, b, c, d)


def hidden_body(own, a_low, a_high, b_low, b_high, o_ref):
    for n, (a, b) in enumerate(((a_low, b_low), (a_high, b_high))):
        rows = slice(n * 64, n * 64 + 64)
        total = own[rows, :].astype(F32) + a[...].astype(F32) + b[...].astype(F32)
        square = jnp.sum(total[:, 2 * FFW :], axis=1, keepdims=True) * (1.0 / 64)
        scale = lax.rsqrt(square / D + tiny_eps)
        gate = total[:, :FFW] * scale
        up = total[:, FFW : 2 * FFW] * scale
        o_ref[rows, :] = (gate / (1.0 + jnp.exp(-gate)) * up).astype(BF)


def hidden_of(*parts):
    return pl.pallas_call(
        hidden_body,
        out_shape=shape((128, FFW)),
        in_specs=[VMEM] * 5,
        out_specs=VMEM,
        compiler_params=params(),
    )(*parts)


def down_body(ids, h0, h1, h2, h3, w_own, w_sib, o_ref, h_ref, w_ref, sems):
    groups = column_copies(w_own, w_sib, w_ref, sems, 576)
    for s, h in enumerate((h0, h1, h2, h3)):
        h_ref[(ids[0] - s) & 3] = h[...]
    for n, (at, end) in enumerate(SPANS):
        finished(groups[n])
        out = dot(h_ref[...].reshape(512, FFW), w_ref[:, at:end]).astype(BF)
        o_ref[:, :, at:end] = out.reshape(CHIPS, 32, end - at)


def down(ids, hs, w_own, w_sib):
    return pl.pallas_call(
        down_body,
        out_shape=shape((CHIPS, 32, DCOL)),
        in_specs=[SMEM] + [VMEM] * 4 + [HBM] * 2,
        out_specs=VMEM,
        scratch_shapes=[
            pltpu.VMEM((4, 128, FFW), BF),
            pltpu.VMEM((FFW, DCOL), BF),
            pltpu.SemaphoreType.DMA((2, 2)),
        ],
        compiler_params=params(),
    )(ids, *hs, w_own, w_sib)


def finish_body(r_ref, m_ref, o_ref):
    total = m_ref[...]
    for k in range(CHIPS):
        total = total + r_ref[k].astype(F32)
    o_ref[...] = total.astype(BF)


def finish(received, mixed):
    return pl.pallas_call(
        finish_body,
        out_shape=shape((32, DCOL)),
        in_specs=[VMEM] * 2,
        out_specs=VMEM,
        compiler_params=params(),
    )(received, mixed)


def route(dz, dx, flip):
    pairs = []
    for z in range(4):
        for x in range(4):
            for core in range(2):
                to = (z + dz) % 4 * 8 + (x + dx) % 4 * 2 + (core ^ flip)
                pairs.append((z * 8 + x * 2 + core, to))
    return pairs


def sent(block, dz=0, dx=0, flip=0):
    return lax.ppermute(block, "dp", route(dz, dx, flip))


def turned(block, s):
    return lax.ppermute(block, "grp", [(i, (i + s) % 4) for i in range(4)])


def traded(blocks):
    same_core = [list(range(core, 32, 2)) for core in range(2)]
    return lax.all_to_all(blocks, "dp", 0, 0, tiled=True, axis_index_groups=same_core)


def blocked(fresh):
    fresh = jnp.pad(fresh, ((0, 0), (0, 16 - STEPS), (0, 5 * HEADS - KW)))
    return fresh.reshape(2, 16, 5, HEADS).transpose(0, 2, 1, 3).reshape(2, FROWS, HEADS)


def on_device(
    queries,
    new_latent,
    latent_cache,
    block_table,
    lengths,
    migration,
    residual,
    value_projection_weight,
    output_proj,
    norm_gain,
    gate_proj,
    up_proj,
    down_projection_matrix,
):
    dp = lax.axis_index("dp")
    grp = lax.axis_index("grp")
    ids = jnp.stack([grp, dp // 8, dp // 2 % 4, dp % 2, dp * 4 + grp, grp, grp, grp]).astype(jnp.int32)
    queries = queries.transpose(0, 1, 3, 2).reshape(2, TROWS, HEADS)
    fresh = blocked(new_latent)
    gain = norm_gain.reshape(1, DCOL)
    places = lax.dynamic_slice_in_dim(migration, dp * 4, 4)
    places = places.reshape(4, 1, 1)
    rows = residual.reshape(4, 2, STEPS, DCOL)
    low, high = rows[:, 0], rows[:, 1]
    rows = jnp.stack([jnp.where(places == 0, high, low), jnp.where(places == 0, low, high)])
    rows = rows.reshape(32, DCOL)

    arrived = sent(pack(ids, migration, queries, fresh), dz=2)
    value_sib = sent(value_projection_weight, flip=1)
    out_sib = sent(output_proj, flip=1)
    gate, up = gate_proj.T, up_proj.T
    gate_sib = sent(gate, flip=1)
    up_sib = sent(up, flip=1)
    down_sib = sent(down_projection_matrix, flip=1)

    def attention(moved, queries, fresh, after):
        return attend(moved, ids, migration, block_table, lengths, queries, fresh, latent_cache, after)

    def project(moved, latent, after):
        return value(moved, ids, latent, value_projection_weight, value_sib, after)

    def spread(block):
        return [block] + [turned(block, s) for s in (1, 2, 3)]

    k_lat = attention(False, queries, fresh, [])
    k_lat_in = traded(k_lat)
    m_lat = attention(True, arrived, arrived, [k_lat])
    m_lat_in = traded(m_lat)
    k_heads = project(False, k_lat_in, [m_lat])
    m_heads = project(True, m_lat_in, [k_heads])
    partial = mix(ids, spread(k_heads), spread(m_heads), output_proj, out_sib)
    mixed, scaled = norm(traded(partial), rows, gain)
    own, a_low, a_high, c_low, c_high, b_low, b_high = gate_up(
        ids, traded(scaled), (gate, gate_sib, up, up_sib)
    )
    c_low, c_high = turned(c_low, 1), turned(c_high, 3)
    a_high, b_low = turned(a_high, 1), turned(b_low, 3)
    a_low, b_high = pass_on(a_low, c_low, b_high, c_high)
    a_low, b_high = turned(a_low, 1), turned(b_high, 3)
    hid = spread(hidden_of(own, a_low, a_high, b_low, b_high))
    partial = down(ids, hid, down_projection_matrix, down_sib)
    out = finish(traded(partial), mixed).reshape(2, 4, STEPS, DCOL)
    out = jnp.stack([jnp.where(places == j, out[1], out[0]) for j in range(2)], axis=1)
    return out.reshape(8, STEPS, DCOL)


def solution(mesh):
    placed = (
        P(("dp", "grp"), None, None, None),
        P(("dp", "grp"), None, None),
        P(("dp", "grp"), None, None),
        P(("dp", "grp"), None),
        P(),
        P(),
        P("dp", None, "grp"),
        P("dp", None, None),
        P("dp", "grp"),
        P("grp"),
        P("grp", "dp"),
        P("grp", "dp"),
        P("dp", "grp"),
    )
    return jax.shard_map(
        on_device, mesh=mesh, in_specs=placed, out_specs=P("dp", None, "grp"), check_vma=False
    )
```

```python
import functools

import jax
import jax.numpy as jnp
from jax import lax
from jax.experimental import pallas as pl
from jax.experimental.pallas import tpu as pltpu
from jax.sharding import PartitionSpec as P

D = 7168
KV = 512
KW = 576
PAGE = 64
MAXP = 32
STEPS = 4
HEADS = 128
TOKENS = PAGE * MAXP
BLOCK = 256
CHUNK = 512
KEYS = TOKENS + 128
QROWS = STEPS * HEADS
TROWS = STEPS * KW
FROWS = 5 * 16
CHIPS = 16
DCOL = D // 4
FFW = 1152
GW = 2 * FFW + 128

score_scale = 0.07216878364870323
exp2_scale = score_scale * 1.4426950408889634
tiny_eps = 1e-06
neg_fill = -1e30

BF = jnp.bfloat16
F32 = jnp.float32
VMEM = pl.BlockSpec(memory_space=pltpu.VMEM)
SMEM = pl.BlockSpec(memory_space=pltpu.SMEM)
ANY = pl.BlockSpec(memory_space=pl.ANY)
HBM = pl.BlockSpec(memory_space=pltpu.HBM)


def params(mb=48):
    return pltpu.CompilerParams(vmem_limit_bytes=mb * 1024 * 1024)


def shape(dims, kind=BF):
    return jax.ShapeDtypeStruct(dims, kind)


def dot(a, b):
    return jnp.dot(a, b, preferred_element_type=F32)


def dot_t(a, b):
    return lax.dot_general(a, b, (((1,), (1,)), ((), ())), preferred_element_type=F32)


def pack_body(ids, mig, q_ref, f_ref, o_ref):
    o_ref[0, :TROWS, :] = q_ref[0]
    o_ref[0, TROWS:, :] = f_ref[0]


def pack(ids, migration, queries, fresh):
    return pl.pallas_call(
        pack_body,
        out_shape=shape((1, TROWS + FROWS, HEADS)),
        grid_spec=pltpu.PrefetchScalarGridSpec(
            num_scalar_prefetch=2,
            grid=(1,),
            in_specs=[
                pl.BlockSpec((1, TROWS, HEADS), lambda i, ids, mig: (mig[ids[4]], 0, 0)),
                pl.BlockSpec((1, FROWS, HEADS), lambda i, ids, mig: (mig[ids[4]], 0, 0)),
            ],
            out_specs=pl.BlockSpec((1, TROWS + FROWS, HEADS), lambda i, ids, mig: (0, 0, 0)),
        ),
        compiler_params=params(),
    )(ids, migration, queries, fresh)


def copy_of(source, target, sem):
    return pltpu.make_async_copy(source, target, sem)


def start(copies):
    for copy in copies:
        copy.start()


def finished(copies):
    for copy in copies:
        copy.wait()


def attend_body(moved, ids, mig, table, lengths, q_ref, f_ref, cache, *refs):
    o_ref, kbuf, t_buf, f_buf, q_buf, sems, i_sems = refs[-7:]
    own = mig[ids[4]]
    row = own if moved else 1 - own
    slot = 0 if moved else row
    inputs = [
        copy_of(q_ref.at[slot, pl.ds(0, TROWS), :], t_buf, i_sems.at[0]),
        copy_of(f_ref.at[slot, pl.ds(TROWS if moved else 0, FROWS), :], f_buf, i_sems.at[1]),
    ]
    start(inputs)
    length = lengths[ids[4] * 2 + row]
    per = CHUNK // PAGE
    groups = [
        [
            copy_of(cache.at[table[row, i]], kbuf.at[pl.ds(i * PAGE, PAGE), :], sems.at[i])
            for i in range(c * per, (c + 1) * per)
        ]
        for c in range(TOKENS // CHUNK)
    ]
    start(groups[0])
    start(groups[1])
    eye = lax.broadcasted_iota(jnp.int32, (HEADS, HEADS), 0)
    eye = (eye == lax.broadcasted_iota(jnp.int32, (HEADS, HEADS), 1)).astype(BF)
    kbuf[TOKENS + 16 :, :] = jnp.zeros((KEYS - TOKENS - 16, KW), BF)
    finished(inputs)
    for i in range(5):
        width = min(HEADS, KW - i * HEADS)
        kbuf[TOKENS : TOKENS + 16, i * HEADS : i * HEADS + width] = f_buf[i * 16 : i * 16 + 16, :width]
    for t in range(STEPS):
        q_buf[t * HEADS : (t + 1) * HEADS, :] = dot_t(eye, t_buf[t * KW : (t + 1) * KW, :]).astype(BF)
    key = lax.broadcasted_iota(jnp.int32, (8, TOKENS), 1)
    past = jnp.where(key < length, 0.0, neg_fill)[0:1]
    place = lax.broadcasted_iota(jnp.int32, (BLOCK, 128), 1)
    step = lax.broadcasted_iota(jnp.int32, (BLOCK, 128), 0) // HEADS
    blocks = []
    for n in range(QROWS // BLOCK):
        q = q_buf[n * BLOCK : (n + 1) * BLOCK, :]
        fresh = dot_t(q, kbuf[TOKENS:, :])
        scores = [jnp.where(place <= step + n * (BLOCK // HEADS), fresh, neg_fill)]
        for c, group in enumerate(groups):
            if n == 0:
                finished(group)
                if c + 2 < len(groups):
                    start(groups[c + 2])
            keys = slice(c * CHUNK, (c + 1) * CHUNK)
            scores.append(dot_t(q, kbuf[keys, :]) + past[:, keys])
        blocks.append(scores)
    for n, scores in enumerate(blocks):
        top = functools.reduce(jnp.maximum, [jnp.max(s, axis=1, keepdims=True) for s in scores])
        weights = [jnp.exp2((s - top) * exp2_scale) for s in scores]
        total = functools.reduce(jnp.add, [jnp.sum(w, axis=1, keepdims=True) for w in weights])
        weight = jnp.concatenate([w.astype(BF) for w in weights[1:] + weights[:1]], axis=1)
        out = dot(weight, kbuf[:, :KV]) / total
        for k in range(CHIPS):
            parts = [out[t * HEADS + k * 8 : t * HEADS + k * 8 + 8] for t in range(BLOCK // HEADS)]
            o_ref[k, n * 16 : n * 16 + 16, :] = jnp.concatenate(parts, axis=0).astype(BF)


def attend(moved, ids, migration, table, lengths, queries, fresh, cache, after):
    return pl.pallas_call(
        functools.partial(attend_body, moved),
        out_shape=shape((CHIPS, 32, KV)),
        in_specs=[SMEM] * 4 + [HBM] * 3 + [ANY] * len(after),
        out_specs=VMEM,
        scratch_shapes=[
            pltpu.VMEM((KEYS, KW), BF),
            pltpu.VMEM((TROWS, HEADS), BF),
            pltpu.VMEM((FROWS, HEADS), BF),
            pltpu.VMEM((QROWS, KW), BF),
            pltpu.SemaphoreType.DMA((MAXP,)),
            pltpu.SemaphoreType.DMA((2,)),
        ],
        compiler_params=params(),
    )(ids, migration, table, lengths, queries, fresh, cache, *after)


def value_body(moved, ids, r_ref, w_own, w_sib, *refs):
    o_ref = refs[-1]
    core = ids[3]
    half = CHIPS // 2
    w = jnp.concatenate([w_own[h] for h in range(4)] + [w_sib[h] for h in range(4)], axis=1)
    head = lax.broadcasted_iota(jnp.int32, (256, 1024), 0) % 8
    place = lax.broadcasted_iota(jnp.int32, (256, 1024), 1) // 128
    meant = head == (place + 4 * core) % 8
    pick = lax.broadcasted_iota(jnp.int32, (32, 256), 1) // 8
    pick = (pick == lax.broadcasted_iota(jnp.int32, (32, 256), 0)).astype(BF)
    for n in range(2):
        at = (1 - n if moved else n) * half
        y = dot(r_ref[at : at + half].reshape(256, KV), w)
        y = jnp.where(meant, y, 0.0).astype(BF)
        o_ref[n * 32 : (n + 1) * 32, :] = dot(pick, y).astype(BF)


def value(moved, ids, received, w_own, w_sib, after):
    return pl.pallas_call(
        functools.partial(value_body, moved),
        out_shape=shape((64, 1024)),
        in_specs=[SMEM, VMEM, VMEM, VMEM] + [ANY] * len(after),
        out_specs=VMEM,
        compiler_params=params(),
    )(ids, received, w_own, w_sib, *after)


SPANS = ((0, 768), (768, 1792))


def column_copies(w_own, w_sib, w_ref, sems, depth):
    groups = []
    for n, (at, end) in enumerate(SPANS):
        cols = pl.ds(at, end - at)
        groups.append(
            [
                copy_of(w.at[:, cols], w_ref.at[pl.ds(i * depth, depth), cols], sems.at[n, i])
                for i, w in enumerate((w_own, w_sib))
            ]
        )
        start(groups[-1])
    return groups


def mix_body(ids, k0, k1, k2, k3, m0, m1, m2, m3, w_own, w_sib, o_ref, h_ref, p_ref, w_ref, sems):
    groups = column_copies(w_own, w_sib, w_ref, sems, 512)
    to = lax.broadcasted_iota(jnp.int32, (256, 256), 0)
    of = lax.broadcasted_iota(jnp.int32, (256, 256), 1)
    order = ((to // 4 % 4) * 64 + (to // 16) * 4 + to % 4 == of).astype(BF)
    for n, hs in enumerate(((k0, k1, k2, k3), (m0, m1, m2, m3))):
        for s, h in enumerate(hs):
            h_ref[(ids[0] - s) & 3] = h[...]
        p_ref[n * 256 : (n + 1) * 256, :] = dot(order, h_ref[...].reshape(256, 1024)).astype(BF)
    for n, (at, end) in enumerate(SPANS):
        finished(groups[n])
        out = dot(p_ref[...], w_ref[:, at:end]).astype(BF)
        o_ref[:, :16, at:end] = out[:256].reshape(CHIPS, 16, end - at)
        o_ref[:, 16:, at:end] = out[256:].reshape(CHIPS, 16, end - at)


def mix(ids, kept, moved, w_own, w_sib):
    return pl.pallas_call(
        mix_body,
        out_shape=shape((CHIPS, 32, DCOL)),
        in_specs=[SMEM] + [VMEM] * 8 + [HBM] * 2,
        out_specs=VMEM,
        scratch_shapes=[
            pltpu.VMEM((4, 64, 1024), BF),
            pltpu.VMEM((512, 1024), BF),
            pltpu.VMEM((1024, DCOL), BF),
            pltpu.SemaphoreType.DMA((2, 2)),
        ],
        compiler_params=params(),
    )(ids, *kept, *moved, w_own, w_sib)


def norm_body(r_ref, res, gain, m_ref, o_ref):
    mixed = res[...].astype(F32)
    for k in range(CHIPS):
        mixed = mixed + r_ref[k].astype(F32)
    m_ref[...] = mixed
    scaled = (mixed * gain[...].astype(F32)).astype(BF)
    square = jnp.sum(mixed * mixed, axis=1, keepdims=True)
    high = square.astype(BF).astype(F32)
    lane = lax.broadcasted_iota(jnp.int32, (32, 128), 1)
    square = jnp.where(lane < 64, high, square - high).astype(BF)
    for k in range(CHIPS):
        o_ref[k, :, :DCOL] = scaled
        o_ref[k, :, DCOL:] = square


def norm(received, residual, gain):
    return pl.pallas_call(
        norm_body,
        out_shape=(shape((32, DCOL), F32), shape((CHIPS, 32, DCOL + 128))),
        in_specs=[VMEM] * 3,
        out_specs=(VMEM,) * 2,
        compiler_params=params(),
    )(received, residual, gain)


PIECES = ((0, 0, 128), (1, 0, 64), (1, 64, 128), (2, 0, 64), (2, 64, 128), (3, 0, 64), (3, 64, 128))


def gate_up_body(ids, x_in, g_own, g_sib, u_own, u_sib, *refs):
    outs, x_ref = refs[: len(PIECES)], refs[len(PIECES)]
    for s in range(4):
        first = ((ids[0] + s) & 3) * 4
        for i in range(4):
            x_ref[s * 128 + i * 32 : s * 128 + i * 32 + 32, :] = x_in[first + i]
    x = x_ref[:, :DCOL]
    for n, (own, sib) in enumerate(((g_own, g_sib), (u_own, u_sib))):
        rest = jnp.concatenate([own[512:, :], sib[512:, :]], axis=0)
        at = n * FFW
        for w in (own[:512, :], sib[:512, :], rest):
            cols = slice(at, at + w.shape[0])
            out = dot_t(x, w).astype(BF)
            for piece, (s, top, end) in zip(outs, PIECES):
                piece[:, cols] = out[s * 128 + top : s * 128 + end]
            at += w.shape[0]
    for piece, (s, top, end) in zip(outs, PIECES):
        piece[:, 2 * FFW :] = x_ref[s * 128 + top : s * 128 + end, DCOL:]


def gate_up(ids, x, weights):
    return pl.pallas_call(
        gate_up_body,
        out_shape=tuple(shape((end - top, GW)) for _, top, end in PIECES),
        in_specs=[SMEM] + [VMEM] * 5,
        out_specs=(VMEM,) * len(PIECES),
        scratch_shapes=[pltpu.VMEM((512, DCOL + 128), BF)],
        compiler_params=params(32),
    )(ids, x, *weights)


def pass_body(a, b, c, d, o_ref, p_ref):
    o_ref[...] = (a[...].astype(F32) + b[...].astype(F32)).astype(BF)
    p_ref[...] = (c[...].astype(F32) + d[...].astype(F32)).astype(BF)


def pass_on(a, b, c, d):
    return pl.pallas_call(
        pass_body,
        out_shape=(shape((64, GW)),) * 2,
        in_specs=[VMEM] * 4,
        out_specs=(VMEM,) * 2,
        compiler_params=params(),
    )(a, b, c, d)


def hidden_body(own, a_low, a_high, b_low, b_high, o_ref):
    for n, (a, b) in enumerate(((a_low, b_low), (a_high, b_high))):
        rows = slice(n * 64, n * 64 + 64)
        total = own[rows, :].astype(F32) + a[...].astype(F32) + b[...].astype(F32)
        square = jnp.sum(total[:, 2 * FFW :], axis=1, keepdims=True) * (1.0 / 64)
        scale = lax.rsqrt(square / D + tiny_eps)
        gate = total[:, :FFW] * scale
        up = total[:, FFW : 2 * FFW] * scale
        o_ref[rows, :] = (gate / (1.0 + jnp.exp(-gate)) * up).astype(BF)


def hidden_of(*parts):
    return pl.pallas_call(
        hidden_body,
        out_shape=shape((128, FFW)),
        in_specs=[VMEM] * 5,
        out_specs=VMEM,
        compiler_params=params(),
    )(*parts)


def down_body(ids, h0, h1, h2, h3, w_own, w_sib, o_ref, h_ref, w_ref, sems):
    groups = column_copies(w_own, w_sib, w_ref, sems, 576)
    for s, h in enumerate((h0, h1, h2, h3)):
        h_ref[(ids[0] - s) & 3] = h[...]
    for n, (at, end) in enumerate(SPANS):
        finished(groups[n])
        h = h_ref[...].reshape(512, FFW)
        rest = jnp.concatenate([w_ref[512:576, at:end], w_ref[1088:, at:end]], axis=0)
        out = dot(h[:, :512], w_ref[:512, at:end]) + dot(h[:, 512:1024], w_ref[576:1088, at:end])
        out = (out + dot(h[:, 1024:], rest)).astype(BF)
        o_ref[:, :, at:end] = out.reshape(CHIPS, 32, end - at)


def down(ids, hs, w_own, w_sib):
    return pl.pallas_call(
        down_body,
        out_shape=shape((CHIPS, 32, DCOL)),
        in_specs=[SMEM] + [VMEM] * 4 + [HBM] * 2,
        out_specs=VMEM,
        scratch_shapes=[
            pltpu.VMEM((4, 128, FFW), BF),
            pltpu.VMEM((FFW, DCOL), BF),
            pltpu.SemaphoreType.DMA((2, 2)),
        ],
        compiler_params=params(),
    )(ids, *hs, w_own, w_sib)


def finish_body(r_ref, m_ref, o_ref):
    total = m_ref[...]
    for k in range(CHIPS):
        total = total + r_ref[k].astype(F32)
    o_ref[...] = total.astype(BF)


def finish(received, mixed):
    return pl.pallas_call(
        finish_body,
        out_shape=shape((32, DCOL)),
        in_specs=[VMEM] * 2,
        out_specs=VMEM,
        compiler_params=params(),
    )(received, mixed)


def route(dz, dx, flip):
    pairs = []
    for z in range(4):
        for x in range(4):
            for core in range(2):
                to = (z + dz) % 4 * 8 + (x + dx) % 4 * 2 + (core ^ flip)
                pairs.append((z * 8 + x * 2 + core, to))
    return pairs


def sent(block, dz=0, dx=0, flip=0):
    return lax.ppermute(block, "dp", route(dz, dx, flip))


def turned(block, s):
    return lax.ppermute(block, "grp", [(i, (i + s) % 4) for i in range(4)])


def traded(blocks):
    same_core = [list(range(core, 32, 2)) for core in range(2)]
    return lax.all_to_all(blocks, "dp", 0, 0, tiled=True, axis_index_groups=same_core)


def blocked(fresh):
    fresh = jnp.pad(fresh, ((0, 0), (0, 16 - STEPS), (0, 5 * HEADS - KW)))
    return fresh.reshape(2, 16, 5, HEADS).transpose(0, 2, 1, 3).reshape(2, FROWS, HEADS)


def on_device(
    queries,
    new_latent,
    latent_cache,
    block_table,
    lengths,
    migration,
    residual,
    value_projection_weight,
    output_proj,
    norm_gain,
    gate_proj,
    up_proj,
    down_projection_matrix,
):
    dp = lax.axis_index("dp")
    grp = lax.axis_index("grp")
    ids = jnp.stack([grp, dp // 8, dp // 2 % 4, dp % 2, dp * 4 + grp, grp, grp, grp]).astype(jnp.int32)
    queries = queries.transpose(0, 1, 3, 2).reshape(2, TROWS, HEADS)
    fresh = blocked(new_latent)
    gain = norm_gain.reshape(1, DCOL)
    places = lax.dynamic_slice_in_dim(migration, dp * 4, 4)
    places = places.reshape(4, 1, 1)
    rows = residual.reshape(4, 2, STEPS, DCOL)
    low, high = rows[:, 0], rows[:, 1]
    rows = jnp.stack([jnp.where(places == 0, high, low), jnp.where(places == 0, low, high)])
    rows = rows.reshape(32, DCOL)

    arrived = sent(pack(ids, migration, queries, fresh), dz=2)
    value_sib = sent(value_projection_weight, flip=1)
    out_sib = sent(output_proj, flip=1)
    gate, up = gate_proj.T, up_proj.T
    gate_sib = sent(gate, flip=1)
    up_sib = sent(up, flip=1)
    down_sib = sent(down_projection_matrix, flip=1)

    def attention(moved, queries, fresh, after):
        return attend(moved, ids, migration, block_table, lengths, queries, fresh, latent_cache, after)

    def project(moved, latent, after):
        return value(moved, ids, latent, value_projection_weight, value_sib, after)

    def spread(block):
        return [block] + [turned(block, s) for s in (1, 2, 3)]

    k_lat = attention(False, queries, fresh, [])
    k_lat_in = traded(k_lat)
    m_lat = attention(True, arrived, arrived, [k_lat])
    m_lat_in = traded(m_lat)
    k_heads = project(False, k_lat_in, [m_lat])
    m_heads = project(True, m_lat_in, [k_heads])
    partial = mix(ids, spread(k_heads), spread(m_heads), output_proj, out_sib)
    mixed, scaled = norm(traded(partial), rows, gain)
    own, a_low, a_high, c_low, c_high, b_low, b_high = gate_up(
        ids, traded(scaled), (gate, gate_sib, up, up_sib)
    )
    c_low, c_high = turned(c_low, 1), turned(c_high, 3)
    a_high, b_low = turned(a_high, 1), turned(b_low, 3)
    a_low, b_high = pass_on(a_low, c_low, b_high, c_high)
    a_low, b_high = turned(a_low, 1), turned(b_high, 3)
    hid = spread(hidden_of(own, a_low, a_high, b_low, b_high))
    partial = down(ids, hid, down_projection_matrix, down_sib)
    out = finish(traded(partial), mixed).reshape(2, 4, STEPS, DCOL)
    out = jnp.stack([jnp.where(places == j, out[1], out[0]) for j in range(2)], axis=1)
    return out.reshape(8, STEPS, DCOL)


def solution(mesh):
    placed = (
        P(("dp", "grp"), None, None, None),
        P(("dp", "grp"), None, None),
        P(("dp", "grp"), None, None),
        P(("dp", "grp"), None),
        P(),
        P(),
        P("dp", None, "grp"),
        P("dp", None, None),
        P("dp", "grp"),
        P("grp"),
        P("grp", "dp"),
        P("grp", "dp"),
        P("dp", "grp"),
    )
    return jax.shard_map(
        on_device, mesh=mesh, in_specs=placed, out_specs=P("dp", None, "grp"), check_vma=False
    )
```

```python
import functools

import jax
import jax.numpy as jnp
from jax import lax
from jax.experimental import pallas as pl
from jax.experimental.pallas import tpu as pltpu
from jax.sharding import PartitionSpec as P

D = 7168
KV = 512
KW = 576
PAGE = 64
MAXP = 32
STEPS = 4
HEADS = 128
TOKENS = PAGE * MAXP
BLOCK = 256
CHUNK = 512
KEYS = TOKENS + 128
QROWS = STEPS * HEADS
TROWS = STEPS * KW
FROWS = 5 * 16
CHIPS = 16
DCOL = D // 4
FFW = 1152
GW = 2 * FFW + 128

score_scale = 0.07216878364870323
exp2_scale = score_scale * 1.4426950408889634
tiny_eps = 1e-06
neg_fill = -1e30

BF = jnp.bfloat16
F32 = jnp.float32
VMEM = pl.BlockSpec(memory_space=pltpu.VMEM)
SMEM = pl.BlockSpec(memory_space=pltpu.SMEM)
ANY = pl.BlockSpec(memory_space=pl.ANY)
HBM = pl.BlockSpec(memory_space=pltpu.HBM)


def params(mb=48):
    return pltpu.CompilerParams(vmem_limit_bytes=mb * 1024 * 1024)


def shape(dims, kind=BF):
    return jax.ShapeDtypeStruct(dims, kind)


def dot(a, b):
    return jnp.dot(a, b, preferred_element_type=F32)


def dot_t(a, b):
    return lax.dot_general(a, b, (((1,), (1,)), ((), ())), preferred_element_type=F32)


def pack_body(ids, mig, q_ref, f_ref, o_ref):
    o_ref[0, :TROWS, :] = q_ref[0]
    o_ref[0, TROWS:, :] = f_ref[0]


def pack(ids, migration, queries, fresh):
    return pl.pallas_call(
        pack_body,
        out_shape=shape((1, TROWS + FROWS, HEADS)),
        grid_spec=pltpu.PrefetchScalarGridSpec(
            num_scalar_prefetch=2,
            grid=(1,),
            in_specs=[
                pl.BlockSpec((1, TROWS, HEADS), lambda i, ids, mig: (mig[ids[4]], 0, 0)),
                pl.BlockSpec((1, FROWS, HEADS), lambda i, ids, mig: (mig[ids[4]], 0, 0)),
            ],
            out_specs=pl.BlockSpec((1, TROWS + FROWS, HEADS), lambda i, ids, mig: (0, 0, 0)),
        ),
        compiler_params=params(),
    )(ids, migration, queries, fresh)


def copy_of(source, target, sem):
    return pltpu.make_async_copy(source, target, sem)


def start(copies):
    for copy in copies:
        copy.start()


def finished(copies):
    for copy in copies:
        copy.wait()


def attend_body(moved, ids, mig, table, lengths, q_ref, f_ref, cache, *refs):
    o_ref, kbuf, t_buf, f_buf, q_buf, sems, i_sems = refs[-7:]
    own = mig[ids[4]]
    row = own if moved else 1 - own
    slot = 0 if moved else row
    inputs = [
        copy_of(q_ref.at[slot, pl.ds(0, TROWS), :], t_buf, i_sems.at[0]),
        copy_of(f_ref.at[slot, pl.ds(TROWS if moved else 0, FROWS), :], f_buf, i_sems.at[1]),
    ]
    start(inputs)
    length = lengths[ids[4] * 2 + row]
    per = CHUNK // PAGE
    groups = [
        [
            copy_of(cache.at[table[row, i]], kbuf.at[pl.ds(i * PAGE, PAGE), :], sems.at[i])
            for i in range(c * per, (c + 1) * per)
        ]
        for c in range(TOKENS // CHUNK)
    ]
    start(groups[0])
    start(groups[1])
    eye = lax.broadcasted_iota(jnp.int32, (HEADS, HEADS), 0)
    eye = (eye == lax.broadcasted_iota(jnp.int32, (HEADS, HEADS), 1)).astype(BF)
    kbuf[TOKENS + 16 :, :] = jnp.zeros((KEYS - TOKENS - 16, KW), BF)
    finished(inputs)
    for i in range(5):
        width = min(HEADS, KW - i * HEADS)
        kbuf[TOKENS : TOKENS + 16, i * HEADS : i * HEADS + width] = f_buf[i * 16 : i * 16 + 16, :width]
    for t in range(STEPS):
        q_buf[t * HEADS : (t + 1) * HEADS, :] = dot_t(eye, t_buf[t * KW : (t + 1) * KW, :]).astype(BF)
    key = lax.broadcasted_iota(jnp.int32, (8, TOKENS), 1)
    past = jnp.where(key < length, 0.0, neg_fill)[0:1]
    place = lax.broadcasted_iota(jnp.int32, (BLOCK, 128), 1)
    step = lax.broadcasted_iota(jnp.int32, (BLOCK, 128), 0) // HEADS
    blocks = []
    for n in range(QROWS // BLOCK):
        q = q_buf[n * BLOCK : (n + 1) * BLOCK, :]
        fresh = dot_t(q, kbuf[TOKENS:, :])
        scores = [jnp.where(place <= step + n * (BLOCK // HEADS), fresh, neg_fill)]
        for c, group in enumerate(groups):
            if n == 0:
                finished(group)
                if c + 2 < len(groups):
                    start(groups[c + 2])
            keys = slice(c * CHUNK, (c + 1) * CHUNK)
            scores.append(dot_t(q, kbuf[keys, :]) + past[:, keys])
        blocks.append(scores)
    for n, scores in enumerate(blocks):
        top = functools.reduce(jnp.maximum, [jnp.max(s, axis=1, keepdims=True) for s in scores])
        weights = [jnp.exp2((s - top) * exp2_scale) for s in scores]
        total = functools.reduce(jnp.add, [jnp.sum(w, axis=1, keepdims=True) for w in weights])
        weight = jnp.concatenate([w.astype(BF) for w in weights[1:] + weights[:1]], axis=1)
        out = dot(weight, kbuf[:, :KV]) / total
        for k in range(CHIPS):
            parts = [out[t * HEADS + k * 8 : t * HEADS + k * 8 + 8] for t in range(BLOCK // HEADS)]
            o_ref[k, n * 16 : n * 16 + 16, :] = jnp.concatenate(parts, axis=0).astype(BF)


def attend(moved, ids, migration, table, lengths, queries, fresh, cache, after):
    return pl.pallas_call(
        functools.partial(attend_body, moved),
        out_shape=shape((CHIPS, 32, KV)),
        in_specs=[SMEM] * 4 + [HBM] * 3 + [ANY] * len(after),
        out_specs=VMEM,
        scratch_shapes=[
            pltpu.VMEM((KEYS, KW), BF),
            pltpu.VMEM((TROWS, HEADS), BF),
            pltpu.VMEM((FROWS, HEADS), BF),
            pltpu.VMEM((QROWS, KW), BF),
            pltpu.SemaphoreType.DMA((MAXP,)),
            pltpu.SemaphoreType.DMA((2,)),
        ],
        compiler_params=params(),
    )(ids, migration, table, lengths, queries, fresh, cache, *after)


def value_body(moved, ids, r_ref, w_own, w_sib, *refs):
    o_ref = refs[-1]
    core = ids[3]
    half = CHIPS // 2
    w = jnp.concatenate([w_own[h] for h in range(4)] + [w_sib[h] for h in range(4)], axis=1)
    head = lax.broadcasted_iota(jnp.int32, (256, 1024), 0) % 8
    place = lax.broadcasted_iota(jnp.int32, (256, 1024), 1) // 128
    meant = head == (place + 4 * core) % 8
    pick = lax.broadcasted_iota(jnp.int32, (32, 256), 1) // 8
    pick = (pick == lax.broadcasted_iota(jnp.int32, (32, 256), 0)).astype(BF)
    for n in range(2):
        at = (1 - n if moved else n) * half
        y = dot(r_ref[at : at + half].reshape(256, KV), w)
        y = jnp.where(meant, y, 0.0).astype(BF)
        o_ref[n * 32 : (n + 1) * 32, :] = dot(pick, y).astype(BF)


def value(moved, ids, received, w_own, w_sib, after):
    return pl.pallas_call(
        functools.partial(value_body, moved),
        out_shape=shape((64, 1024)),
        in_specs=[SMEM, VMEM, VMEM, VMEM] + [ANY] * len(after),
        out_specs=VMEM,
        compiler_params=params(),
    )(ids, received, w_own, w_sib, *after)


SPANS = ((0, 768), (768, 1792))


def column_copies(w_own, w_sib, w_ref, sems, depth):
    groups = []
    for n, (at, end) in enumerate(SPANS):
        cols = pl.ds(at, end - at)
        groups.append(
            [
                copy_of(w.at[:, cols], w_ref.at[pl.ds(i * depth, depth), cols], sems.at[n, i])
                for i, w in enumerate((w_own, w_sib))
            ]
        )
        start(groups[-1])
    return groups


def mix_body(ids, k0, k1, k2, k3, m0, m1, m2, m3, w_own, w_sib, o_ref, h_ref, p_ref, w_ref, sems):
    groups = column_copies(w_own, w_sib, w_ref, sems, 512)
    to = lax.broadcasted_iota(jnp.int32, (256, 256), 0)
    of = lax.broadcasted_iota(jnp.int32, (256, 256), 1)
    order = ((to // 4 % 4) * 64 + (to // 16) * 4 + to % 4 == of).astype(BF)
    for n, hs in enumerate(((k0, k1, k2, k3), (m0, m1, m2, m3))):
        for s, h in enumerate(hs):
            h_ref[(ids[0] - s) & 3] = h[...]
        p_ref[n * 256 : (n + 1) * 256, :] = dot(order, h_ref[...].reshape(256, 1024)).astype(BF)
    for n, (at, end) in enumerate(SPANS):
        finished(groups[n])
        out = dot(p_ref[...], w_ref[:, at:end]).astype(BF)
        o_ref[:, :16, at:end] = out[:256].reshape(CHIPS, 16, end - at)
        o_ref[:, 16:, at:end] = out[256:].reshape(CHIPS, 16, end - at)


def mix(ids, kept, moved, w_own, w_sib):
    return pl.pallas_call(
        mix_body,
        out_shape=shape((CHIPS, 32, DCOL)),
        in_specs=[SMEM] + [VMEM] * 8 + [HBM] * 2,
        out_specs=VMEM,
        scratch_shapes=[
            pltpu.VMEM((4, 64, 1024), BF),
            pltpu.VMEM((512, 1024), BF),
            pltpu.VMEM((1024, DCOL), BF),
            pltpu.SemaphoreType.DMA((2, 2)),
        ],
        compiler_params=params(),
    )(ids, *kept, *moved, w_own, w_sib)


def norm_body(r_ref, res, gain, m_ref, o_ref):
    mixed = res[...].astype(F32)
    for k in range(CHIPS):
        mixed = mixed + r_ref[k].astype(F32)
    m_ref[...] = mixed
    scaled = (mixed * gain[...].astype(F32)).astype(BF)
    square = jnp.sum(mixed * mixed, axis=1, keepdims=True)
    high = square.astype(BF).astype(F32)
    lane = lax.broadcasted_iota(jnp.int32, (32, 128), 1)
    square = jnp.where(lane < 64, high, square - high).astype(BF)
    for k in range(CHIPS):
        o_ref[k, :, :DCOL] = scaled
        o_ref[k, :, DCOL:] = square


def norm(received, residual, gain):
    return pl.pallas_call(
        norm_body,
        out_shape=(shape((32, DCOL), F32), shape((CHIPS, 32, DCOL + 128))),
        in_specs=[VMEM] * 3,
        out_specs=(VMEM,) * 2,
        compiler_params=params(),
    )(received, residual, gain)


PIECES = ((0, 0, 128), (1, 0, 64), (1, 64, 128), (2, 0, 64), (2, 64, 128), (3, 0, 64), (3, 64, 128))


FF_SPANS = ((0, 256), (256, 1280), (1280, 2 * FFW))


def gate_up_body(ids, x_in, g_own, g_sib, u_own, u_sib, *refs):
    outs, (x_ref, w_ref, sems) = refs[: len(PIECES)], refs[len(PIECES) :]
    groups = []
    for at, end in FF_SPANS:
        group = []
        while at < end:
            which, row = divmod(at, 576)
            count = min(end - at, 576 - row)
            source = (g_own, g_sib, u_own, u_sib)[which].at[pl.ds(row, count), :]
            group.append(copy_of(source, w_ref.at[pl.ds(at, count), :], sems.at[len(groups), len(group)]))
            at += count
        groups.append(group)
    start(groups[0])
    start(groups[1])
    for s in range(4):
        first = ((ids[0] + s) & 3) * 4
        for i in range(4):
            x_ref[s * 128 + i * 32 : s * 128 + i * 32 + 32, :] = x_in[first + i]
    for n, (at, end) in enumerate(FF_SPANS):
        finished(groups[n])
        if n + 2 < len(groups):
            start(groups[n + 2])
        cols = slice(at, end)
        out = dot_t(x_ref[:, :DCOL], w_ref[cols, :]).astype(BF)
        for piece, (s, top, end) in zip(outs, PIECES):
            piece[:, cols] = out[s * 128 + top : s * 128 + end]
    for piece, (s, top, end) in zip(outs, PIECES):
        piece[:, 2 * FFW :] = x_ref[s * 128 + top : s * 128 + end, DCOL:]


def gate_up(ids, x, weights):
    return pl.pallas_call(
        gate_up_body,
        out_shape=tuple(shape((end - top, GW)) for _, top, end in PIECES),
        in_specs=[SMEM, VMEM] + [HBM] * 4,
        out_specs=(VMEM,) * len(PIECES),
        scratch_shapes=[
            pltpu.VMEM((512, DCOL + 128), BF),
            pltpu.VMEM((2 * FFW, DCOL), BF),
            pltpu.SemaphoreType.DMA((len(FF_SPANS), 3)),
        ],
        compiler_params=params(),
    )(ids, x, *weights)


def pass_body(a, b, c, d, o_ref, p_ref):
    o_ref[...] = (a[...].astype(F32) + b[...].astype(F32)).astype(BF)
    p_ref[...] = (c[...].astype(F32) + d[...].astype(F32)).astype(BF)


def pass_on(a, b, c, d):
    return pl.pallas_call(
        pass_body,
        out_shape=(shape((64, GW)),) * 2,
        in_specs=[VMEM] * 4,
        out_specs=(VMEM,) * 2,
        compiler_params=params(),
    )(a, b, c, d)


def hidden_body(own, a_low, a_high, b_low, b_high, o_ref):
    for n, (a, b) in enumerate(((a_low, b_low), (a_high, b_high))):
        rows = slice(n * 64, n * 64 + 64)
        total = own[rows, :].astype(F32) + a[...].astype(F32) + b[...].astype(F32)
        square = jnp.sum(total[:, 2 * FFW :], axis=1, keepdims=True) * (1.0 / 64)
        scale = lax.rsqrt(square / D + tiny_eps)
        gate = total[:, :FFW] * scale
        up = total[:, FFW : 2 * FFW] * scale
        o_ref[rows, :] = (gate / (1.0 + jnp.exp(-gate)) * up).astype(BF)


def hidden_of(*parts):
    return pl.pallas_call(
        hidden_body,
        out_shape=shape((128, FFW)),
        in_specs=[VMEM] * 5,
        out_specs=VMEM,
        compiler_params=params(),
    )(*parts)


def down_body(ids, h0, h1, h2, h3, w_own, w_sib, o_ref, h_ref, w_ref, sems):
    groups = column_copies(w_own, w_sib, w_ref, sems, 576)
    for s, h in enumerate((h0, h1, h2, h3)):
        h_ref[(ids[0] - s) & 3] = h[...]
    for n, (at, end) in enumerate(SPANS):
        finished(groups[n])
        out = dot(h_ref[...].reshape(512, FFW), w_ref[:, at:end]).astype(BF)
        o_ref[:, :, at:end] = out.reshape(CHIPS, 32, end - at)


def down(ids, hs, w_own, w_sib):
    return pl.pallas_call(
        down_body,
        out_shape=shape((CHIPS, 32, DCOL)),
        in_specs=[SMEM] + [VMEM] * 4 + [HBM] * 2,
        out_specs=VMEM,
        scratch_shapes=[
            pltpu.VMEM((4, 128, FFW), BF),
            pltpu.VMEM((FFW, DCOL), BF),
            pltpu.SemaphoreType.DMA((2, 2)),
        ],
        compiler_params=params(),
    )(ids, *hs, w_own, w_sib)


def finish_body(r_ref, m_ref, o_ref):
    total = m_ref[...]
    for k in range(CHIPS):
        total = total + r_ref[k].astype(F32)
    o_ref[...] = total.astype(BF)


def finish(received, mixed):
    return pl.pallas_call(
        finish_body,
        out_shape=shape((32, DCOL)),
        in_specs=[VMEM] * 2,
        out_specs=VMEM,
        compiler_params=params(),
    )(received, mixed)


def route(dz, dx, flip):
    pairs = []
    for z in range(4):
        for x in range(4):
            for core in range(2):
                to = (z + dz) % 4 * 8 + (x + dx) % 4 * 2 + (core ^ flip)
                pairs.append((z * 8 + x * 2 + core, to))
    return pairs


def sent(block, dz=0, dx=0, flip=0):
    return lax.ppermute(block, "dp", route(dz, dx, flip))


def turned(block, s):
    return lax.ppermute(block, "grp", [(i, (i + s) % 4) for i in range(4)])


def traded(blocks):
    same_core = [list(range(core, 32, 2)) for core in range(2)]
    return lax.all_to_all(blocks, "dp", 0, 0, tiled=True, axis_index_groups=same_core)


def blocked(fresh):
    fresh = jnp.pad(fresh, ((0, 0), (0, 16 - STEPS), (0, 5 * HEADS - KW)))
    return fresh.reshape(2, 16, 5, HEADS).transpose(0, 2, 1, 3).reshape(2, FROWS, HEADS)


def on_device(
    queries,
    new_latent,
    latent_cache,
    block_table,
    lengths,
    migration,
    residual,
    value_projection_weight,
    output_proj,
    norm_gain,
    gate_proj,
    up_proj,
    down_projection_matrix,
):
    dp = lax.axis_index("dp")
    grp = lax.axis_index("grp")
    ids = jnp.stack([grp, dp // 8, dp // 2 % 4, dp % 2, dp * 4 + grp, grp, grp, grp]).astype(jnp.int32)
    queries = queries.transpose(0, 1, 3, 2).reshape(2, TROWS, HEADS)
    fresh = blocked(new_latent)
    gain = norm_gain.reshape(1, DCOL)
    places = lax.dynamic_slice_in_dim(migration, dp * 4, 4)
    places = places.reshape(4, 1, 1)
    rows = residual.reshape(4, 2, STEPS, DCOL)
    low, high = rows[:, 0], rows[:, 1]
    rows = jnp.stack([jnp.where(places == 0, high, low), jnp.where(places == 0, low, high)])
    rows = rows.reshape(32, DCOL)

    arrived = sent(pack(ids, migration, queries, fresh), dz=2)
    value_sib = sent(value_projection_weight, flip=1)
    out_sib = sent(output_proj, flip=1)
    gate, up = gate_proj.T, up_proj.T
    gate_sib = sent(gate, flip=1)
    up_sib = sent(up, flip=1)
    down_sib = sent(down_projection_matrix, flip=1)

    def attention(moved, queries, fresh, after):
        return attend(moved, ids, migration, block_table, lengths, queries, fresh, latent_cache, after)

    def project(moved, latent, after):
        return value(moved, ids, latent, value_projection_weight, value_sib, after)

    def spread(block):
        return [block] + [turned(block, s) for s in (1, 2, 3)]

    k_lat = attention(False, queries, fresh, [])
    k_lat_in = traded(k_lat)
    m_lat = attention(True, arrived, arrived, [k_lat])
    m_lat_in = traded(m_lat)
    k_heads = project(False, k_lat_in, [m_lat])
    m_heads = project(True, m_lat_in, [k_heads])
    partial = mix(ids, spread(k_heads), spread(m_heads), output_proj, out_sib)
    mixed, scaled = norm(traded(partial), rows, gain)
    own, a_low, a_high, c_low, c_high, b_low, b_high = gate_up(
        ids, traded(scaled), (gate, gate_sib, up, up_sib)
    )
    c_low, c_high = turned(c_low, 1), turned(c_high, 3)
    a_high, b_low = turned(a_high, 1), turned(b_low, 3)
    a_low, b_high = pass_on(a_low, c_low, b_high, c_high)
    a_low, b_high = turned(a_low, 1), turned(b_high, 3)
    hid = spread(hidden_of(own, a_low, a_high, b_low, b_high))
    partial = down(ids, hid, down_projection_matrix, down_sib)
    out = finish(traded(partial), mixed).reshape(2, 4, STEPS, DCOL)
    out = jnp.stack([jnp.where(places == j, out[1], out[0]) for j in range(2)], axis=1)
    return out.reshape(8, STEPS, DCOL)


def solution(mesh):
    placed = (
        P(("dp", "grp"), None, None, None),
        P(("dp", "grp"), None, None),
        P(("dp", "grp"), None, None),
        P(("dp", "grp"), None),
        P(),
        P(),
        P("dp", None, "grp"),
        P("dp", None, None),
        P("dp", "grp"),
        P("grp"),
        P("grp", "dp"),
        P("grp", "dp"),
        P("dp", "grp"),
    )
    return jax.shard_map(
        on_device, mesh=mesh, in_specs=placed, out_specs=P("dp", None, "grp"), check_vma=False
    )
```
